32 devices in a mesh: seq: 16 (over z, y, x), head: 2 (over core).
Axes of the slice: x: 2, y: 2, z: 4, core: 2. Of those that a mesh axis runs over, the one named last changes fastest.
Arguments:
- layer_input: bfloat16 [8192, 2048], P('seq'), may hold values from -6 to 6
- seq_lengths: int32 [4], replicated, may hold values from 1 to 7936, as said below
- gain_attn: bfloat16 [2048], P('seq'), may hold values from 0.5 to 1.5
- w_query: bfloat16 [2048, 256], P('seq', 'head'), may hold values from -0.125 to 0.125
- w_key: bfloat16 [2048, 256], P('seq', 'head'), may hold values from -0.125 to 0.125
- w_value: bfloat16 [2048, 2048], P('seq', 'head'), may hold values from -0.125 to 0.125
- w_out: bfloat16 [2048, 2048], P('head', 'seq'), may hold values from -1 to 1
- gain_mlp: bfloat16 [2048], P('seq'), may hold values from 0.5 to 1.5
- w_gate: bfloat16 [2048, 5632], P('seq', 'head'), may hold values from -0.125 to 0.125
- w_up: bfloat16 [2048, 5632], P('seq', 'head'), may hold values from -0.125 to 0.125
- w_down: bfloat16 [5632, 2048], P('head', 'seq'), may hold values from -0.078125 to 0.078125
- cotangent: bfloat16 [8192, 2048], P('seq'), may hold values from -6 to 6
Outputs:
- layer_out: bfloat16 [8192, 2048], P('seq')
- input_grad: float32 [8192, 2048], P('seq')
- gain_attn_grad: float32 [2048], P('seq')
- w_query_grad: float32 [2048, 256], P('seq', 'head')
- w_key_grad: float32 [2048, 256], P('seq', 'head')
- w_value_grad: float32 [2048, 2048], P('seq', 'head')
- w_out_grad: float32 [2048, 2048], P('head', 'seq')
- gain_mlp_grad: float32 [2048], P('seq')
- w_gate_grad: float32 [2048, 5632], P('seq', 'head')
- w_up_grad: float32 [2048, 5632], P('seq', 'head')
- w_down_grad: float32 [5632, 2048], P('head', 'seq')
- den_stats: float32 [2], replicated
The draws below stay inside these ranges and needn't reach their ends.
Inputs may be any that keep to these rules, and one draw needn't show every extreme that they name: `seq_lengths`: the sequences fill all 8192 positions; the longest has exactly 7936 positions.
All inputs are finite; a program needn't handle non-finite values.
Results may differ from the reference program's by a relative error of at most 0.012.
Values may be sent and summed in bfloat16 or wider, within the bound.
A program may use at most 256 MiB of HBM per device.

```python
import math
import jax
import jax.numpy as jnp
from jax import lax

D = 2048
H = 16
FD = 16
DV = 128
FF = 5632
NSEQ = 4
TOKENS = 8192
LONGEST = 7936


def draw_seq_lengths(key, part):
    remain = TOKENS - LONGEST
    key_cut = jax.random.fold_in(key, 11)
    key_place = jax.random.fold_in(key, 23)
    order = jax.random.permutation(key_cut, jnp.arange(1, remain, dtype=jnp.int32))
    cuts = jnp.sort(order[:NSEQ - 2]).astype(jnp.int32)
    edges = jnp.concatenate([jnp.zeros((1,), jnp.int32), cuts, jnp.full((1,), remain, jnp.int32)])
    others = edges[1:] - edges[:-1]
    where_long = jax.random.randint(key_place, (), 0, NSEQ, dtype=jnp.int32)
    slots = jnp.arange(NSEQ, dtype=jnp.int32)
    source = jnp.clip(jnp.where(slots < where_long, slots, slots - 1), 0, NSEQ - 2)
    picked = jnp.take(others, source)
    return jnp.where(slots == where_long, LONGEST, picked).astype(jnp.int32)


def block_levels(own_key, extent, split, smallest, top_value):
    level = 1.0
    for position, parts in split:
        draws = jax.random.uniform(jax.random.fold_in(jax.random.fold_in(own_key, 6), position), (parts,), jnp.float32, smallest / len(split), top_value / len(split))
        level = level * jnp.repeat(jnp.exp(draws), extent[position] // parts).reshape((-1,) + (1,) * (len(extent) - 1 - position))
    return level


def centred(key, extent, scale, reach, split=(), held_as=jnp.bfloat16):
    drawn = scale * jax.random.normal(key, extent, jnp.float32)
    if split:
        drawn = drawn * block_levels(key, extent, split, -0.22, 0.18)
    return jnp.clip(drawn, -reach, reach).astype(held_as)


def setup_inputs(seed: int = 0) -> dict:
    arg_keys = jax.random.split(jax.random.key(seed), 13)
    layer_input = centred(arg_keys[0], (TOKENS, D), 1.0, 6.0, ((0, 16),))
    seq_lengths = draw_seq_lengths(jax.random.fold_in(arg_keys[12], 71), 0)
    gain_attn = jnp.clip(1.0 + 0.1 * jax.random.normal(arg_keys[2], (D,), jnp.float32), 0.5, 1.5).astype(jnp.bfloat16)
    w_query = centred(arg_keys[3], (D, H * FD), D ** -0.5, 0.125, ((0, 16), (1, 2)))
    w_key = centred(arg_keys[4], (D, H * FD), D ** -0.5, 0.125, ((0, 16), (1, 2)))
    w_value = centred(arg_keys[5], (D, H * DV), D ** -0.5, 0.125, ((0, 16), (1, 2)))
    w_out = centred(arg_keys[6], (H * DV, D), (max(1, H * DV // 64)) ** -0.5, 1.0, ((0, 2), (1, 16)))
    gain_mlp = jnp.clip(1.0 + 0.1 * jax.random.normal(arg_keys[7], (D,), jnp.float32), 0.5, 1.5).astype(jnp.bfloat16)
    w_gate = centred(arg_keys[8], (D, FF), D ** -0.5, 0.125, ((0, 16), (1, 2)))
    w_up = centred(arg_keys[9], (D, FF), D ** -0.5, 0.125, ((0, 16), (1, 2)))
    w_down = centred(arg_keys[10], (FF, D), FF ** -0.5, 0.078125, ((0, 2), (1, 16)))
    cotangent = centred(arg_keys[11], (TOKENS, D), 1.0, 6.0, ((0, 16),))
    return dict(layer_input=layer_input, seq_lengths=seq_lengths, gain_attn=gain_attn, w_query=w_query, w_key=w_key, w_value=w_value, w_out=w_out, gain_mlp=gain_mlp, w_gate=w_gate, w_up=w_up, w_down=w_down, cotangent=cotangent)


@jax.custom_vjp
def low(v):
    return lax.optimization_barrier(v.astype(jnp.bfloat16)).astype(jnp.float32)

@jax.custom_vjp
def low_back(v):
    return v

def low_keep(v):
    return (low(v), None)

def low_pass(kept, grad):
    return (grad,)

def back_keep(v):
    return (v, None)

def back_low(kept, grad):
    return (low(grad),)
low.defvjp(low_keep, low_pass)
low_back.defvjp(back_keep, back_low)
HIGH = lax.Precision.HIGHEST

def features(vectors):
    feat_width = vectors.shape[-1]
    outer_prod = (vectors[..., :, None] * vectors[..., None, :]).reshape(vectors.shape[:-1] + (feat_width * feat_width,))
    ones_col = jnp.ones(vectors.shape[:-1] + (1,), vectors.dtype)
    return jnp.concatenate([ones_col, vectors * feat_width ** (-0.25), outer_prod * (feat_width ** (-0.5) / math.sqrt(2.0))], axis=-1)

def segment_starts(seq_lengths, positions):
    seq_starts = jnp.cumsum(seq_lengths) - seq_lengths
    picked = jnp.where(seq_starts[None, :] <= positions[:, None], seq_starts[None, :], 0)
    return lax.optimization_barrier(jnp.max(picked, axis=1)).astype(jnp.int32)

def rms_norm(values, gain_vec):
    return values * lax.rsqrt(lax.optimization_barrier(jnp.mean(values * values, axis=-1, keepdims=True)) + 1e-05) * gain_vec

def mat_prod(left, right):
    return jnp.dot(left, right, precision=HIGH, preferred_element_type=jnp.float32)

def attend(query, key_rows, value_rows, seg_start):
    block = math.gcd(TOKENS, 512)
    count = TOKENS // block
    scale_root = FD ** 0.5
    query_blocks = query.reshape(count, block, H, FD)
    key_blocks = key_rows.reshape(count, block, H, FD)
    value_blocks = value_rows.reshape(count, block, H, DV)
    start_blocks = seg_start.reshape(count, block)
    block_firsts = (jnp.arange(count) * block).astype(jnp.int32)

    def step(carry, item):
        state, norm_sum = carry
        query_b, key_b, value_b, start_b, block_first = item
        local_pos = jnp.arange(block)
        causal = (local_pos[None, :] <= local_pos[:, None]) & (start_b[None, :] == start_b[:, None])
        scores = jnp.einsum('thd,uhd->htu', query_b, key_b, precision=HIGH) / scale_root
        weights = jnp.where(causal[None], 1.0 + scores + 0.5 * scores * scores, 0.0)
        carried = (start_b < block_first).astype(query_b.dtype)
        query_feat = features(query_b) * carried[:, None, None]
        numer = jnp.einsum('htu,uhv->thv', weights, value_b, precision=HIGH)
        numer = numer + jnp.einsum('thf,hfv->thv', query_feat, state, precision=HIGH)
        denom = lax.optimization_barrier(jnp.sum(weights, axis=-1)).T + jnp.einsum('thf,hf->th', query_feat, norm_sum, precision=HIGH)
        tail_mask = (start_b == start_b[-1]).astype(query_b.dtype)
        key_feat = features(key_b) * tail_mask[:, None, None]
        keep_prev = 1.0 - (start_b[-1] >= block_first).astype(query_b.dtype)
        state = jnp.einsum('thf,thv->hfv', key_feat, value_b, precision=HIGH) + keep_prev * state
        norm_sum = lax.optimization_barrier(jnp.sum(key_feat, axis=0)) + keep_prev * norm_sum
        return ((state, norm_sum), (numer / denom[..., None], denom))
    feat_count = 1 + FD + FD * FD
    init = (jnp.zeros((H, feat_count, DV), query.dtype), jnp.zeros((H, feat_count), query.dtype))
    _, (mixed, denom) = lax.scan(jax.checkpoint(step), init, (query_blocks, key_blocks, value_blocks, start_blocks, block_firsts))
    return (mixed.reshape(TOKENS, H * DV), denom.reshape(TOKENS, H))

def reference(layer_input, seq_lengths, gain_attn, w_query, w_key, w_value, w_out, gain_mlp, w_gate, w_up, w_down, cotangent):
    positions = jnp.arange(TOKENS, dtype=jnp.int32)
    seg_start = segment_starts(seq_lengths, positions)

    def layer(x_float, gain_one, query_w, key_w, value_w, out_w, gain_two, gate_w, up_w, down_w):
        normed_attn = low(rms_norm(x_float, gain_one))
        query = low(low_back(mat_prod(normed_attn, query_w))).reshape(TOKENS, H, FD)
        key_rows = low(low_back(mat_prod(normed_attn, key_w))).reshape(TOKENS, H, FD)
        value_rows = low(low_back(mat_prod(normed_attn, value_w))).reshape(TOKENS, H, DV)
        mixed, denom = attend(query, key_rows, value_rows, seg_start)
        attn_branch = low_back(mat_prod(low(mixed), out_w))
        resid = x_float + attn_branch
        normed_mlp = low(rms_norm(resid, gain_two))
        gate = low_back(mat_prod(normed_mlp, gate_w))
        up_proj = low_back(mat_prod(normed_mlp, up_w))
        hidden = low(jax.nn.silu(gate) * up_proj)
        return (resid + low_back(mat_prod(hidden, down_w)), denom)
    primals = tuple((item.astype(jnp.float32) for item in (layer_input, gain_attn, w_query, w_key, w_value, w_out, gain_mlp, w_gate, w_up, w_down)))
    layer_out, pull_back, denom = jax.vjp(layer, *primals, has_aux=True)
    grads = pull_back(cotangent.astype(jnp.float32))
    den_stats = jnp.stack([jnp.log(jnp.min(denom)), jnp.log(jnp.max(denom))])
    return (layer_out.astype(jnp.bfloat16), grads[0], grads[1], grads[2], grads[3], grads[4], grads[5], grads[6], grads[7], grads[8], grads[9], den_stats)
```

```python
import functools
import math

import jax
import jax.numpy as jnp
import numpy as np
from jax import lax
from jax.experimental import pallas as pl
from jax.experimental.pallas import tpu as pltpu
from jax.sharding import PartitionSpec as P

H = 16
FD = 16
DV = 128
PLANE = 4
FE = 160
F32, BF = jnp.float32, jnp.bfloat16
NN = (((1,), (0,)), ((), ()))
NT = (((1,), (1,)), ((), ()))
TN = (((0,), (0,)), ((), ()))
LANE_ONE = 64
VMEM = 48 * 2**20


def dot(a, b, dims=NN):
    return lax.dot_general(a, b, dims, preferred_element_type=F32)


def feature_maps():
    qa, qb, ka, kb = (np.zeros((2, 128, FE), np.float32) for _ in range(4))
    q_to_k, k_to_q = (np.zeros((2, 128, 128), np.float32) for _ in range(2))
    for h in range(2):
        q0, k0, f = h * FD, 2 * FD + h * FD, 0
        for i in range(FD):
            for j in range(i, FD):
                qa[h, q0 + i, f] = 1 / 32 if i == j else 1 / 16
                qb[h, q0 + j, f] = 1
                ka[h, k0 + i, f] = kb[h, k0 + j, f] = 1
                f += 1
        for i in range(FD):
            qa[h, q0 + i, f], qb[h, LANE_ONE, f] = 1 / 4, 1
            ka[h, k0 + i, f] = kb[h, LANE_ONE, f] = 1
            f += 1
            q_to_k[h, q0 + i, k0 + i] = k_to_q[h, k0 + i, q0 + i] = 1 / 4
        for m in (qa, qb, ka, kb):
            m[h, LANE_ONE, f] = 1
    wide = [np.pad(m, ((0, 0), (0, 0), (0, 256 - FE))) for m in (qa, qb, ka, kb)]
    one = np.zeros((2, 128, 128), np.float32)
    one[:, LANE_ONE, 0] = 1
    both = np.concatenate([*wide, q_to_k, k_to_q, one], axis=-1)
    return jnp.asarray(both, BF)


def read_maps(maps, h):
    cuts = [(256 * i, FE) for i in range(4)] + [(1024, 128), (1152, 128)]
    return [maps[h, :, a : a + n] for a, n in cuts]


def start_of(sc, n_seq, pos):
    best = jnp.zeros_like(pos)
    for k in range(n_seq):
        at = sc[2 + k]
        best = jnp.where(at <= pos, at, best)
    return best


class Chunk:
    def __init__(self, sc, n_seq, i, rows):
        self.first = sc[1] + i * rows
        self.last = self.first + rows - 1
        pos = self.first + lax.broadcasted_iota(jnp.int32, (rows, 1), 0)
        self.pos = pos
        self.start = start_of(sc, n_seq, pos)
        self.last_start = start_of(sc, n_seq, self.last)
        self.before_start = start_of(sc, n_seq, self.first - 1)
        self.carried = (self.start < self.first).astype(F32)
        self.tail = (self.start == self.last_start).astype(F32)
        self.keep = (self.last_start < self.first).astype(F32)
        self.rows = rows

    def causal(self):
        earlier = self.first + lax.broadcasted_iota(jnp.int32, (self.rows, self.rows), 1)
        return (earlier <= self.pos) & (earlier >= self.start)


def query_key(qkv):
    block = qkv[:, 2 * DV : 3 * DV]
    lane = lax.broadcasted_iota(jnp.int32, block.shape, 1)
    one = jnp.where(lane == LANE_ONE, 1.0, 0.0).astype(BF)
    return jnp.where(lane < LANE_ONE, block, one)


def one_column(qk, maps):
    return dot(qk, maps[0, :, 1280:1408]).astype(BF)


def with_one(value, ones):
    return jnp.concatenate([value, ones], axis=1)


def project_kernel(x_ref, gain_ref, w_ref, normed_ref, qkv_ref):
    x = x_ref[0].astype(F32)
    inv = lax.rsqrt(jnp.mean(x * x, axis=-1, keepdims=True) + 1e-05)
    normed = (x * inv * gain_ref[...]).astype(BF)
    normed_ref[0] = normed
    qkv_ref[0] = dot(normed, w_ref[...]).astype(BF)


def states_kernel(n_seq, sc, qkv_ref, maps, before_ref, total_ref, state):
    i = pl.program_id(0)

    @pl.when(i == 0)
    def _():
        state[...] = jnp.zeros_like(state)

    qkv = qkv_ref[0]
    ch = Chunk(sc, n_seq, i, qkv.shape[0])
    qk = query_key(qkv)
    ones = one_column(qk, maps)
    for h in range(2):
        _, _, ka, kb, _, _ = read_maps(maps, h)
        before_ref[0, h] = state[h].astype(BF)
        feat = (dot(qk, ka) * dot(qk, kb) * ch.tail).astype(BF)
        new = dot(feat, with_one(qkv[:, h * DV : (h + 1) * DV], ones), TN) + ch.keep * state[h]
        state[h] = new
        total_ref[h] = new.astype(BF)


def attend_kernel(n_seq, slot, sc, qkv_ref, before_ref, enter_ref, maps, wo_ref, out1, out0, mixed_ref, den_ref):
    g = pl.program_id(0)
    half = pl.num_programs(0) // 2
    qkv = qkv_ref[0]
    rows = qkv.shape[0]
    ch = Chunk(sc, n_seq, slot(g) ^ sc[0], rows)
    alive = (ch.before_start < sc[1]).astype(F32)
    qk = query_key(qkv)
    ones = one_column(qk, maps)
    causal = ch.causal()
    dens = []
    for h in range(2):
        qa, qb, _, _, q_to_k, _ = read_maps(maps, h)
        s = dot(dot(qk, q_to_k).astype(BF), qk, NT)
        w = jnp.where(causal, 1.0 + s + 0.5 * s * s, 0.0).astype(BF)
        feat = (dot(qk, qa) * dot(qk, qb) * ch.carried).astype(BF)
        state = (before_ref[0, h].astype(F32) + alive * enter_ref[h].astype(F32)).astype(BF)
        num = dot(w, with_one(qkv[:, h * DV : (h + 1) * DV], ones)) + dot(feat, state)
        den = num[:, DV : DV + 1]
        mixed_ref[0, :, h * DV : (h + 1) * DV] = (num[:, :DV] / den).astype(BF)
        dens.append(den)
    lane = lax.broadcasted_iota(jnp.int32, (rows, 128), 1)
    den_ref[0] = jnp.where(lane == 0, dens[0], dens[1])
    part = dot(mixed_ref[0], wo_ref[...], NT).astype(BF)

    @pl.when(g < half)
    def _():
        out1[0] = part

    @pl.when(g >= half)
    def _():
        out0[0] = part


def mlp_kernel(n_ref, cot_ref, wgu_ref, wd_ref, h_ref, ggu_ref, out1, out0):
    g = pl.program_id(0)
    half = pl.num_programs(0) // 2
    main = (wgu_ref.shape[1] - 128) // 2
    gu = dot(n_ref[0], wgu_ref[...])
    gh = dot(cot_ref[0], wd_ref[...], NT)

    def parts(gate, up, grad):
        sig = 1.0 / (1.0 + jnp.exp(-gate))
        silu = gate * sig
        return silu * up, grad * up * sig * (1.0 + gate * (1.0 - sig)), grad * silu

    hid, g_gate, g_up = parts(gu[:, :main], gu[:, main : 2 * main], gh[:, :main])
    h_ref[0, :, :main] = hid.astype(BF)
    ggu_ref[0, :, :main] = g_gate.astype(BF)
    ggu_ref[0, :, main : 2 * main] = g_up.astype(BF)
    rest = gu[:, 2 * main :]
    hid, g_gate, g_up = parts(rest, pltpu.roll(rest, 64, 1), gh[:, main:])
    low = lax.broadcasted_iota(jnp.int32, hid.shape, 1) < 64
    h_ref[0, :, main:] = jnp.where(low, hid, 0.0).astype(BF)
    ggu_ref[0, :, 2 * main :] = jnp.where(low, g_gate, pltpu.roll(g_up, 64, 1)).astype(BF)
    part = dot(ggu_ref[0], wgu_ref[...], NT).astype(BF)

    @pl.when(g < half)
    def _():
        out1[0] = part

    @pl.when(g >= half)
    def _():
        out0[0] = part


def grads_in_kernel(n_seq, sc, ga_ref, wo_ref, qkv_ref, mixed_ref, den_ref, maps, gaug_ref, after_ref, total_ref, state):
    k, n = pl.program_id(0), pl.num_programs(0)
    i = n - 1 - k

    @pl.when(k == 0)
    def _():
        state[...] = jnp.zeros_like(state)

    qkv = qkv_ref[0]
    rows = qkv.shape[0]
    ch = Chunk(sc, n_seq, i, rows)
    qk = query_key(qkv)
    gm = dot(ga_ref[0], wo_ref[...])
    lane = lax.broadcasted_iota(jnp.int32, (rows, 128), 1)
    for h in range(2):
        qa, qb, _, _, _, _ = read_maps(maps, h)
        den = den_ref[0, :, h : h + 1]
        grad = gm[:, h * DV : (h + 1) * DV] / den
        delta = -jnp.sum(grad * mixed_ref[0, :, h * DV : (h + 1) * DV].astype(F32), axis=1, keepdims=True)
        gaug = jnp.concatenate([grad, jnp.where(lane == 0, delta, 0.0)], axis=1).astype(BF)
        gaug_ref[0, :, h * 2 * DV : (h + 1) * 2 * DV] = gaug
        after_ref[0, h] = state[h].astype(BF)
        feat = (dot(qk, qa) * dot(qk, qb) * ch.carried).astype(BF)
        new = dot(feat, gaug, TN) + ch.keep * state[h]
        state[h] = new
        total_ref[h] = new.astype(BF)


def grads_kernel(
    n_seq, slot, sc, qkv_ref, gaug_ref, before_ref, enter_ref, after_ref, leave_ref, maps, w_ref, out1, out0, dqkv_ref
):
    g = pl.program_id(0)
    half = pl.num_programs(0) // 2
    qkv = qkv_ref[0]
    rows = qkv.shape[0]
    ch = Chunk(sc, n_seq, slot(g) ^ sc[0], rows)
    group_last = sc[1] + pl.num_programs(0) * rows - 1
    alive = (ch.before_start < sc[1]).astype(F32)
    alive_after = (start_of(sc, n_seq, group_last) <= ch.last).astype(F32)
    qk = query_key(qkv)
    ones = one_column(qk, maps)
    causal = ch.causal()
    dqk = jnp.zeros((rows, 128), F32)
    for h in range(2):
        qa, qb, ka, kb, q_to_k, k_to_q = read_maps(maps, h)
        value = with_one(qkv[:, h * DV : (h + 1) * DV], ones)
        gaug = gaug_ref[0, :, h * 2 * DV : (h + 1) * 2 * DV]
        quarter = dot(qk, q_to_k).astype(BF)
        s = dot(quarter, qk, NT)
        w = jnp.where(causal, 1.0 + s + 0.5 * s * s, 0.0).astype(BF)
        ds = jnp.where(causal, dot(gaug, value, NT) * (1.0 + s), 0.0).astype(BF)
        dqk += dot(ds, dot(qk, k_to_q).astype(BF)) + dot(ds, quarter, TN)
        before = (before_ref[0, h].astype(F32) + alive * enter_ref[h].astype(F32)).astype(BF)
        after = (after_ref[0, h].astype(F32) + alive_after * leave_ref[h].astype(F32)).astype(BF)
        a, b = dot(qk, qa), dot(qk, qb)
        df = dot(gaug, before, NT) * ch.carried
        dqk += dot((df * b).astype(BF), qa, NT) + dot((df * a).astype(BF), qb, NT)
        a, b = dot(qk, ka), dot(qk, kb)
        df = dot(value, after, NT) * ch.tail
        dqk += dot((df * b).astype(BF), ka, NT) + dot((df * a).astype(BF), kb, NT)
        feat = (a * b * ch.tail).astype(BF)
        dv = dot(w, gaug[:, :DV], TN) + dot(feat, after[:, :DV])
        dqkv_ref[0, :, h * DV : (h + 1) * DV] = dv.astype(BF)
    lane = lax.broadcasted_iota(jnp.int32, dqk.shape, 1)
    dqkv_ref[0, :, 2 * DV :] = jnp.where(lane < LANE_ONE, dqk, 0.0).astype(BF)
    part = dot(dqkv_ref[0], w_ref[...], NT).astype(BF)

    @pl.when(g < half)
    def _():
        out1[0] = part

    @pl.when(g >= half)
    def _():
        out0[0] = part


class Place:
    def __init__(self):
        self.n = lax.axis_size("seq")
        self.groups = self.n // PLANE
        s = lax.axis_index("seq")
        self.s, self.z, self.p, self.c = s, s // PLANE, s % PLANE, lax.axis_index("head")

    def flip(self, v, bits):
        return lax.ppermute(v, "seq", [(s, s ^ bits) for s in range(self.n)])

    def core(self, v):
        return lax.ppermute(v, "head", [(0, 1), (1, 0)])

    def along(self, v, step, sources):
        pairs = [
            (s, s + step * PLANE)
            for s in range(self.n)
            if s // PLANE in sources and 0 <= s // PLANE + step < self.groups
        ]
        return lax.ppermute(v, "seq", pairs)

    def spread(self, pack):
        own = [lax.dynamic_index_in_dim(pack, self.p ^ j, 0, keepdims=False) for j in range(PLANE)]
        got = [own[0]] + [self.flip(own[j], j) for j in range(1, PLANE)]
        return [lax.select_n(self.p, *[got[i ^ q] for q in range(PLANE)]) for i in range(PLANE)]

    def gather_line(self, slab):
        up, down, top = [slab], [slab], self.groups
        for k in range(1, top):
            up.append(self.along(up[-1], 1, range(k - 1, top)))
            down.append(self.along(down[-1], -1, range(0, top - k + 1)))
        return [
            lax.select_n(self.z, *[up[q - i] if q >= i else down[i - q] for q in range(top)]) for i in range(top)
        ]

    def scatter_line(self, piece):
        top = self.groups
        total = piece(self.z).astype(F32)
        for step in (1, -1):
            got = None
            for k in range(1, top):
                far = top - k if step == 1 else k - top
                term = piece(jnp.clip(self.z + far, 0, top - 1))
                if got is not None:
                    term = (term.astype(F32) + got.astype(F32)).astype(BF)
                sources = range(0, k) if step == 1 else range(top - k, top)
                got = self.along(term, step, sources)
            if got is not None:
                total = total + got.astype(F32)
        return total

    def gather8(self, mine, other=None):
        cut = mine.shape[0] // 2
        mx, my = self.flip(mine, 1), self.flip(mine, 2)
        da, db = self.flip(my[:cut], 1), self.flip(mx[cut:], 2)
        other = self.core(mine) if other is None else other
        ox, oy, oda, odb = (self.core(v) for v in (mx, my, da, db))
        whole = jnp.concatenate([mine, other, mx, ox, my, oy, da, db, oda, odb], axis=0)
        return whole.reshape(2 * PLANE, mine.shape[0], mine.shape[1])

    def reduce8(self, other_half, own_half):
        total = own_half.astype(F32) + self.core(other_half).astype(F32)
        cut = total.shape[1] // 2
        a, b = total[:, :cut], total[:, cut:]
        got_x = self.flip(a[1::2].astype(BF), 1).astype(F32)
        got_y = self.flip(b[2:].astype(BF), 2).astype(F32)
        last_y = self.flip((a[2] + got_x[1]).astype(BF), 2).astype(F32)
        last_x = self.flip((b[1] + got_y[1]).astype(BF), 1).astype(F32)
        return jnp.concatenate([a[0] + got_x[0] + last_y, b[0] + got_y[0] + last_x], axis=0)

    def both(self, mine):
        other = self.core(mine)
        return jnp.concatenate(
            [lax.select_n(self.c, mine, other), lax.select_n(self.c, other, mine)], axis=0
        )


def cost(flops, nbytes):
    return pl.CostEstimate(flops=int(flops), bytes_accessed=int(nbytes), transcendentals=0)


def rms_parts(rows):
    return lax.rsqrt(jnp.mean(rows * rows, axis=-1, keepdims=True) + 1e-05)


def rms_back(grad_normed, x_hat, inv_rms, gain_vec):
    grad_hat = grad_normed * gain_vec
    return inv_rms * (grad_hat - x_hat * jnp.mean(grad_hat * x_hat, axis=-1, keepdims=True))


def split_hidden(w):
    rows, cols = w.shape
    main = cols // PLANE // 128 * 128
    rest = (cols - PLANE * main) // PLANE
    first = w[:, : PLANE * main].reshape(rows, PLANE, main)
    return first.transpose(1, 0, 2), w[:, PLANE * main :].reshape(rows, PLANE, rest).transpose(1, 0, 2)


def shards(
    layer_input,
    seq_lengths,
    gain_attn,
    w_query,
    w_key,
    w_value,
    w_out,
    gain_mlp,
    w_gate,
    w_up,
    w_down,
    cotangent,
):
    me = Place()
    rows, width = layer_input.shape
    half_rows = rows // 2
    slots = 2 * PLANE
    group_rows = PLANE * rows
    n_seq = seq_lengths.shape[0]
    db = w_query.shape[0]
    hidden = w_down.shape[0]
    main = hidden // PLANE // 128 * 128
    rest = hidden // PLANE - main
    assert H == slots * 2 and rest == 64
    own8 = me.p * 2 + me.c

    k = jnp.arange(n_seq)
    starts = jnp.sum(jnp.where(k[None, :] < k[:, None], seq_lengths[None, :], 0), axis=1)
    first = me.z * group_rows
    sc = jnp.concatenate([jnp.stack([own8, first]).astype(jnp.int32), starts.astype(jnp.int32)])
    maps = feature_maps()

    def slot_first_other(g):
        return (g % PLANE) * 2 + 1 - g // PLANE

    def by_part(w, parts=PLANE):
        return w.reshape(w.shape[0], parts, w.shape[1] // parts).transpose(1, 0, 2)

    gains = jnp.stack([gain_attn, gain_mlp], axis=1)
    fill = jnp.concatenate([gains, jnp.zeros((db, 62), BF)], axis=1)
    attn_pack = jnp.concatenate(
        [by_part(w_value), by_part(w_query), by_part(w_key), jnp.broadcast_to(fill, (PLANE, db, 64)), by_part(w_out.T)],
        axis=2,
    )
    g_main, g_rest = split_hidden(w_gate)
    u_main, u_rest = split_hidden(w_up)
    gu_pack = jnp.concatenate([g_main, u_main, g_rest, u_rest], axis=2)
    down_pack = jnp.concatenate(
        [w_down[: PLANE * main].reshape(PLANE, main, db), w_down[PLANE * main :].reshape(PLANE, rest, db)], axis=1
    )
    attn_w = jnp.concatenate(me.gather_line(jnp.concatenate(me.spread(attn_pack), axis=0)), axis=0)
    gu_w = jnp.concatenate(me.gather_line(jnp.concatenate(me.spread(gu_pack), axis=0)), axis=0)
    down_w = jnp.concatenate(me.gather_line(jnp.concatenate(me.spread(down_pack), axis=1)), axis=1)
    down_w = jnp.concatenate([down_w, jnp.zeros((64, width), BF)], axis=0)
    w_qkv, w_o = attn_w[:, : 3 * DV], attn_w[:, 3 * DV :]
    gain_one = attn_w[:, 2 * DV + 64].astype(F32)[None, :]
    gain_two = attn_w[:, 2 * DV + 65].astype(F32)[None, :]

    def my_half(v):
        return lax.dynamic_slice_in_dim(v, me.c * half_rows, half_rows, 0)

    def other_half(v):
        return lax.dynamic_slice_in_dim(v, (1 - me.c) * half_rows, half_rows, 0)

    x_all = me.gather8(my_half(layer_input), other_half(layer_input))
    cot_all = me.gather8(my_half(cotangent), other_half(cotangent))

    params = pltpu.CompilerParams(dimension_semantics=("arbitrary",), vmem_limit_bytes=VMEM)
    row_block = lambda cols: pl.BlockSpec((1, half_rows, cols), lambda g: (g, 0, 0))
    whole = lambda *shape: pl.BlockSpec(shape, lambda *_: (0,) * len(shape))

    normed, qkv = pl.pallas_call(
        project_kernel,
        grid=(slots,),
        in_specs=[row_block(width), whole(1, width), whole(width, 3 * DV)],
        out_specs=[row_block(width), row_block(3 * DV)],
        out_shape=[
            jax.ShapeDtypeStruct((slots, half_rows, width), BF),
            jax.ShapeDtypeStruct((slots, half_rows, 3 * DV), BF),
        ],
        compiler_params=params,
        cost_estimate=cost(2 * group_rows * width * 3 * DV, 4 * group_rows * width),
        name="project",
    )(x_all, gain_one, w_qkv)

    map_spec = whole(*maps.shape)
    state_spec = whole(2, FE, 2 * DV)
    state_shape = jax.ShapeDtypeStruct((2, FE, 2 * DV), BF)
    states_shape = jax.ShapeDtypeStruct((slots, 2, FE, 2 * DV), BF)

    def in_order(cols):
        return pl.BlockSpec((1, half_rows, cols), lambda i, s: (i ^ s[0], 0, 0))

    before, total = pl.pallas_call(
        functools.partial(states_kernel, n_seq),
        grid_spec=pltpu.PrefetchScalarGridSpec(
            num_scalar_prefetch=1,
            grid=(slots,),
            in_specs=[in_order(3 * DV), map_spec],
            out_specs=[pl.BlockSpec((1, 2, FE, 2 * DV), lambda i, s: (i, 0, 0, 0)), state_spec],
            scratch_shapes=[pltpu.VMEM((2, FE, 2 * DV), F32)],
        ),
        out_shape=[states_shape, state_shape],
        compiler_params=params,
        cost_estimate=cost(slots * 2e8, 2**21),
        name="states",
    )(sc, qkv, maps)

    def start_at(pos):
        return jnp.max(jnp.where(starts <= pos, starts, 0))

    top = me.groups
    reach = start_at(first - 1)
    enter = jnp.zeros((2, FE, 2 * DV), F32)
    for hop in range(1, top):
        got = me.along(total, hop, range(top)).astype(F32)
        live = (me.z >= hop) & (reach < first - (hop - 1) * group_rows)
        enter = enter + jnp.where(live, got, 0.0)
    enter = enter.astype(BF)

    def any_order(cols):
        return pl.BlockSpec((1, half_rows, cols), lambda g, s: (slot_first_other(g), 0, 0))

    def any_state(g, s):
        return (slot_first_other(g) ^ s[0], 0, 0, 0)

    part_specs = [
        pl.BlockSpec((1, half_rows, width), lambda g, *_: (jnp.minimum(g, PLANE - 1), 0, 0)),
        pl.BlockSpec((1, half_rows, width), lambda g, *_: (jnp.maximum(g - PLANE, 0), 0, 0)),
    ]
    part_shapes = [jax.ShapeDtypeStruct((PLANE, half_rows, width), BF)] * 2
    attn_other, attn_own, mixed, den = pl.pallas_call(
        functools.partial(attend_kernel, n_seq, slot_first_other),
        grid_spec=pltpu.PrefetchScalarGridSpec(
            num_scalar_prefetch=1,
            grid=(slots,),
            in_specs=[
                any_order(3 * DV),
                pl.BlockSpec((1, 2, FE, 2 * DV), any_state),
                state_spec,
                map_spec,
                whole(width, 2 * DV),
            ],
            out_specs=[*part_specs, any_order(2 * DV), any_order(128)],
        ),
        out_shape=[
            *part_shapes,
            jax.ShapeDtypeStruct((slots, half_rows, 2 * DV), BF),
            jax.ShapeDtypeStruct((slots, half_rows, 128), F32),
        ],
        compiler_params=params,
        cost_estimate=cost(slots * 8e8, 2**24),
        name="attend",
    )(sc, qkv, before, enter, maps, w_o)

    x_mine = my_half(layer_input).astype(F32)
    resid = x_mine + me.reduce8(attn_other, attn_own)
    inv_two = rms_parts(resid)
    x_hat_two = resid * inv_two
    normed_mlp = me.gather8((x_hat_two * gain_two).astype(BF))

    wide = 2 * main + 2 * rest
    tall = main + 128
    hid, grad_gu, gn_other, gn_own = pl.pallas_call(
        mlp_kernel,
        grid=(slots,),
        in_specs=[
            pl.BlockSpec((1, half_rows, width), lambda g: (slot_first_other(g), 0, 0)),
            pl.BlockSpec((1, half_rows, width), lambda g: (slot_first_other(g), 0, 0)),
            whole(width, wide),
            whole(tall, width),
        ],
        out_specs=[
            pl.BlockSpec((1, half_rows, tall), lambda g: (slot_first_other(g), 0, 0)),
            pl.BlockSpec((1, half_rows, wide), lambda g: (slot_first_other(g), 0, 0)),
            *part_specs,
        ],
        out_shape=[
            jax.ShapeDtypeStruct((slots, half_rows, tall), BF),
            jax.ShapeDtypeStruct((slots, half_rows, wide), BF),
            *part_shapes,
        ],
        compiler_params=params,
        cost_estimate=cost(2 * group_rows * width * (2 * wide + tall), 2**25),
        name="mlp",
    )(normed_mlp, cot_all, gu_w, down_w)

    grad_normed_mlp = me.reduce8(gn_other, gn_own)
    grad_resid = my_half(cotangent).astype(F32) + rms_back(grad_normed_mlp, x_hat_two, inv_two, gain_two)
    grad_attn = me.gather8(grad_resid.astype(BF))

    def flat(v):
        return v.reshape(slots * half_rows, v.shape[2])

    gu_grad = dot(flat(normed_mlp), flat(grad_gu), TN).astype(BF)
    down_grad = dot(flat(hid), flat(cot_all), TN).astype(BF)
    lo = dot(flat(hid), down_w).astype(BF).reshape(PLANE, 2, half_rows, width)
    mlp_sum = me.reduce8(lo[:, 1], lo[:, 0])
    layer_out = me.both((resid + mlp_sum).astype(BF))

    def reverse(cols):
        return pl.BlockSpec((1, half_rows, cols), lambda k, s: ((slots - 1 - k) ^ s[0], 0, 0))

    gaug, after, back_total = pl.pallas_call(
        functools.partial(grads_in_kernel, n_seq),
        grid_spec=pltpu.PrefetchScalarGridSpec(
            num_scalar_prefetch=1,
            grid=(slots,),
            in_specs=[reverse(width), whole(width, 2 * DV), reverse(3 * DV), reverse(2 * DV), reverse(128), map_spec],
            out_specs=[
                reverse(4 * DV),
                pl.BlockSpec((1, 2, FE, 2 * DV), lambda k, s: (slots - 1 - k, 0, 0, 0)),
                state_spec,
            ],
            scratch_shapes=[pltpu.VMEM((2, FE, 2 * DV), F32)],
        ),
        out_shape=[jax.ShapeDtypeStruct((slots, half_rows, 4 * DV), BF), states_shape, state_shape],
        compiler_params=params,
        cost_estimate=cost(slots * 8e8, 2**24),
        name="grads_in",
    )(sc, grad_attn, w_o, qkv, mixed, den, maps)

    leave = jnp.zeros((2, FE, 2 * DV), F32)
    for hop in range(1, top):
        got = me.along(back_total, -hop, range(top)).astype(F32)
        other_first = first + hop * group_rows
        live = (me.z + hop < top) & (start_at(other_first - 1) < first + group_rows)
        leave = leave + jnp.where(live, got, 0.0)
    leave = leave.astype(BF)

    ga_other, ga_own, dqkv = pl.pallas_call(
        functools.partial(grads_kernel, n_seq, slot_first_other),
        grid_spec=pltpu.PrefetchScalarGridSpec(
            num_scalar_prefetch=1,
            grid=(slots,),
            in_specs=[
                any_order(3 * DV),
                any_order(4 * DV),
                pl.BlockSpec((1, 2, FE, 2 * DV), any_state),
                state_spec,
                pl.BlockSpec((1, 2, FE, 2 * DV), any_state),
                state_spec,
                map_spec,
                whole(width, 3 * DV),
            ],
            out_specs=[*part_specs, any_order(3 * DV)],
        ),
        out_shape=[*part_shapes, jax.ShapeDtypeStruct((slots, half_rows, 3 * DV), BF)],
        compiler_params=params,
        cost_estimate=cost(slots * 16e8, 2**24),
        name="grads",
    )(sc, qkv, gaug, before, enter, after, leave, maps, w_qkv)

    grad_normed = me.reduce8(ga_other, ga_own).astype(BF)
    grad_normed_both = me.both(grad_normed).astype(F32)
    grad_resid_both = me.both(grad_resid)
    x_float = layer_input.astype(F32)
    inv_one = rms_parts(x_float)
    input_grad = grad_resid_both + rms_back(grad_normed_both, x_float * inv_one, inv_one, gain_one)

    qkv_grad = dot(flat(normed), flat(dqkv), TN).astype(BF)
    o_grad = dot(flat(grad_attn), flat(mixed), TN).astype(BF)
    attn_grad = jnp.concatenate([qkv_grad, o_grad], axis=1)
    slab = PLANE * db

    def row_piece(v):
        return lambda i: lax.dynamic_slice_in_dim(v, i * slab, slab, 0)

    def col_piece(v):
        return lambda i: lax.dynamic_slice_in_dim(v, i * slab, slab, 1)

    gu_sum = me.scatter_line(row_piece(gu_grad)).astype(BF)
    down_sum = me.scatter_line(col_piece(down_grad[: main + rest])).astype(BF)
    attn_sum = me.scatter_line(row_piece(attn_grad)).astype(BF)
    gu_parts = me.spread(gu_sum.reshape(PLANE, db, wide))
    down_parts = me.spread(down_sum.reshape(main + rest, PLANE, db).transpose(1, 0, 2))
    attn_parts = me.spread(attn_sum.reshape(PLANE, db, 5 * DV))

    def cols(parts, a, b):
        return [v[:, a:b].astype(F32) for v in parts]

    gate_grad = jnp.concatenate(cols(gu_parts, 0, main) + cols(gu_parts, 2 * main, 2 * main + rest), axis=1)
    up_grad = jnp.concatenate(cols(gu_parts, main, 2 * main) + cols(gu_parts, 2 * main + rest, wide), axis=1)
    down_out = jnp.concatenate(
        [v[:main].astype(F32) for v in down_parts] + [v[main:].astype(F32) for v in down_parts], axis=0
    )
    value_grad = jnp.concatenate(cols(attn_parts, 0, 2 * DV), axis=1)
    query_grad = jnp.concatenate(cols(attn_parts, 2 * DV, 2 * DV + 2 * FD), axis=1)
    key_grad = jnp.concatenate(cols(attn_parts, 2 * DV + 2 * FD, 2 * DV + 4 * FD), axis=1)
    out_grad = jnp.concatenate(cols(attn_parts, 3 * DV, 5 * DV), axis=1).T

    def along_cols(*pairs):
        return sum(jnp.sum(w.astype(F32) * grad, axis=1) for w, grad in pairs)

    gain_parts = jnp.stack(
        [
            along_cols((w_query, query_grad), (w_key, key_grad), (w_value, value_grad)),
            along_cols((w_gate, gate_grad), (w_up, up_grad)),
        ]
    )
    gain_sums = gain_parts + me.core(gain_parts)
    gain_one_grad = gain_sums[0] / gain_attn.astype(F32)
    gain_two_grad = gain_sums[1] / gain_mlp.astype(F32)

    den2 = den[:, :, :2]
    ends = jnp.stack([-jnp.min(den2), jnp.max(den2)])
    ends = jnp.broadcast_to(ends[:, None], (2, 128))
    ends = jnp.maximum(ends, me.core(ends))
    ends = jnp.maximum(ends, me.flip(ends, 1))
    ends = jnp.maximum(ends, me.flip(ends, 2))
    best = ends
    for hop in range(1, top):
        for step in (hop, -hop):
            got = me.along(ends, step, range(top))
            ok = (me.z - step >= 0) & (me.z - step < top)
            best = jnp.where(ok, jnp.maximum(best, got), best)
    den_stats = jnp.stack([jnp.log(-best[0, 0]), jnp.log(best[1, 0])])

    return (
        layer_out,
        input_grad,
        gain_one_grad,
        query_grad,
        key_grad,
        value_grad,
        out_grad,
        gain_two_grad,
        gate_grad,
        up_grad,
        down_out,
        den_stats,
    )


def solution(mesh):
    return jax.shard_map(
        shards,
        mesh=mesh,
        in_specs=(
            P("seq", None),
            P(),
            P("seq"),
            P("seq", "head"),
            P("seq", "head"),
            P("seq", "head"),
            P("head", "seq"),
            P("seq"),
            P("seq", "head"),
            P("seq", "head"),
            P("head", "seq"),
            P("seq", None),
        ),
        out_specs=(
            P("seq", None),
            P("seq", None),
            P("seq"),
            P("seq", "head"),
            P("seq", "head"),
            P("seq", "head"),
            P("head", "seq"),
            P("seq"),
            P("seq", "head"),
            P("seq", "head"),
            P("head", "seq"),
            P(),
        ),
        check_vma=False,
    )
```

```python
import functools
import math

import jax
import jax.numpy as jnp
import numpy as np
from jax import lax
from jax.experimental import pallas as pl
from jax.experimental.pallas import tpu as pltpu
from jax.sharding import PartitionSpec as P

H = 16
FD = 16
DV = 128
PLANE = 4
FE = 160
F32, BF = jnp.float32, jnp.bfloat16
NN = (((1,), (0,)), ((), ()))
NT = (((1,), (1,)), ((), ()))
TN = (((0,), (0,)), ((), ()))
LANE_ONE = 64
VMEM = 48 * 2**20


def dot(a, b, dims=NN):
    return lax.dot_general(a, b, dims, preferred_element_type=F32)


def feature_maps():
    qa, qb, ka, kb = (np.zeros((2, 128, FE), np.float32) for _ in range(4))
    q_to_k, k_to_q = (np.zeros((2, 128, 128), np.float32) for _ in range(2))
    for h in range(2):
        q0, k0, f = h * FD, 2 * FD + h * FD, 0
        for i in range(FD):
            for j in range(i, FD):
                qa[h, q0 + i, f] = 1 / 32 if i == j else 1 / 16
                qb[h, q0 + j, f] = 1
                ka[h, k0 + i, f] = kb[h, k0 + j, f] = 1
                f += 1
        for i in range(FD):
            qa[h, q0 + i, f], qb[h, LANE_ONE, f] = 1 / 4, 1
            ka[h, k0 + i, f] = kb[h, LANE_ONE, f] = 1
            f += 1
            q_to_k[h, q0 + i, k0 + i] = k_to_q[h, k0 + i, q0 + i] = 1 / 4
        for m in (qa, qb, ka, kb):
            m[h, LANE_ONE, f] = 1
    wide = [np.pad(m, ((0, 0), (0, 0), (0, 256 - FE))) for m in (qa, qb, ka, kb)]
    one = np.zeros((2, 128, 128), np.float32)
    one[:, LANE_ONE, 0] = 1
    both = np.concatenate([*wide, q_to_k, k_to_q, one], axis=-1)
    return jnp.asarray(both, BF)


def read_maps(maps, h):
    cuts = [(256 * i, FE) for i in range(4)] + [(1024, 128), (1152, 128)]
    return [maps[h, :, a : a + n] for a, n in cuts]


def start_of(sc, n_seq, pos):
    best = jnp.zeros_like(pos)
    for k in range(n_seq):
        at = sc[2 + k]
        best = jnp.where(at <= pos, at, best)
    return best


class Chunk:
    def __init__(self, sc, n_seq, i, rows):
        self.first = sc[1] + i * rows
        self.last = self.first + rows - 1
        pos = self.first + lax.broadcasted_iota(jnp.int32, (rows, 1), 0)
        self.pos = pos
        self.start = start_of(sc, n_seq, pos)
        self.last_start = start_of(sc, n_seq, self.last)
        self.before_start = start_of(sc, n_seq, self.first - 1)
        self.carried = (self.start < self.first).astype(F32)
        self.tail = (self.start == self.last_start).astype(F32)
        self.keep = (self.last_start < self.first).astype(F32)
        self.rows = rows

    def causal(self):
        earlier = self.first + lax.broadcasted_iota(jnp.int32, (self.rows, self.rows), 1)
        return (earlier <= self.pos) & (earlier >= self.start)


def query_key(qkv):
    block = qkv[:, 2 * DV : 3 * DV]
    lane = lax.broadcasted_iota(jnp.int32, block.shape, 1)
    one = jnp.where(lane == LANE_ONE, 1.0, 0.0).astype(BF)
    return jnp.where(lane < LANE_ONE, block, one)


def one_column(qk, maps):
    return dot(qk, maps[0, :, 1280:1408]).astype(BF)


def with_one(value, ones):
    return jnp.concatenate([value, ones], axis=1)


def project_kernel(x_ref, gain_ref, w_ref, normed_ref, qkv_ref):
    x = x_ref[0].astype(F32)
    inv = lax.rsqrt(jnp.mean(x * x, axis=-1, keepdims=True) + 1e-05)
    normed = (x * inv * gain_ref[...]).astype(BF)
    normed_ref[0] = normed
    qkv_ref[0] = dot(normed, w_ref[...]).astype(BF)


def states_kernel(n_seq, sc, qkv_ref, maps, before_ref, total_ref, state):
    i = pl.program_id(0)

    @pl.when(i == 0)
    def _():
        state[...] = jnp.zeros_like(state)

    qkv = qkv_ref[0]
    ch = Chunk(sc, n_seq, i, qkv.shape[0])
    qk = query_key(qkv)
    ones = one_column(qk, maps)
    for h in range(2):
        _, _, ka, kb, _, _ = read_maps(maps, h)
        before_ref[0, h] = state[h].astype(BF)
        feat = (dot(qk, ka) * dot(qk, kb) * ch.tail).astype(BF)
        new = dot(feat, with_one(qkv[:, h * DV : (h + 1) * DV], ones), TN) + ch.keep * state[h]
        state[h] = new
        total_ref[h] = new.astype(BF)


def attend_kernel(n_seq, slot, sc, qkv_ref, before_ref, enter_ref, maps, wo_ref, out1, out0, mixed_ref, den_ref):
    g = pl.program_id(0)
    half = pl.num_programs(0) // 2
    qkv = qkv_ref[0]
    rows = qkv.shape[0]
    ch = Chunk(sc, n_seq, slot(g) ^ sc[0], rows)
    alive = (ch.before_start < sc[1]).astype(F32)
    qk = query_key(qkv)
    ones = one_column(qk, maps)
    causal = ch.causal()
    dens = []
    for h in range(2):
        qa, qb, _, _, q_to_k, _ = read_maps(maps, h)
        s = dot(dot(qk, q_to_k).astype(BF), qk, NT)
        w = jnp.where(causal, 1.0 + s + 0.5 * s * s, 0.0).astype(BF)
        feat = (dot(qk, qa) * dot(qk, qb) * ch.carried).astype(BF)
        state = (before_ref[0, h].astype(F32) + alive * enter_ref[h].astype(F32)).astype(BF)
        num = dot(w, with_one(qkv[:, h * DV : (h + 1) * DV], ones)) + dot(feat, state)
        den = num[:, DV : DV + 1]
        mixed_ref[0, :, h * DV : (h + 1) * DV] = (num[:, :DV] / den).astype(BF)
        dens.append(den)
    lane = lax.broadcasted_iota(jnp.int32, (rows, 128), 1)
    den_ref[0] = jnp.where(lane == 0, dens[0], dens[1])
    part = dot(mixed_ref[0], wo_ref[...], NT).astype(BF)

    @pl.when(g < half)
    def _():
        out1[0] = part

    @pl.when(g >= half)
    def _():
        out0[0] = part


def line_blocks(z, top, near, far, slab):
    found = [(None, z, near[0])]
    for k in range(1, top):
        for sign in (-1, 1):
            at = z + sign * k
            i = 2 * k - (sign < 0)
            src = near[i] if i < len(near) else rows_of(far, jnp.clip(at, 0, top - 1), slab)
            found.append(((at >= 0) & (at < top), at, src))
    return found


def mlp_kernel(
    top, n_ref, cot_ref, g0, gu1, gd1, gu2, gd2, g_far, d0, du1, dd1, d_far,
    h_ref, ggu_ref, out1, out0, dw_out, wgu_ref, wd_ref, sems, out_sem,
):
    g = pl.program_id(0)
    half = pl.num_programs(0) // 2
    slab = g0.shape[0]
    z = lax.div(lax.axis_index("seq"), PLANE)

    @pl.when(g == 0)
    def _():
        copies = []
        for ref, near, far in ((wgu_ref, (g0, gu1, gd1, gu2, gd2), g_far), (wd_ref, (d0, du1, dd1), d_far)):
            for cond, block, src in line_blocks(z, top, near, far, slab):

                def copy(ref=ref, block=block, src=src, i=len(copies)):
                    return pltpu.make_async_copy(src, rows_of(ref, block, slab), sems.at[i])

                copies.append((cond, copy))
        for what in ("start", "wait"):
            for cond, copy in copies:
                if cond is None:
                    getattr(copy(), what)()
                else:
                    pl.when(cond)(lambda copy=copy: getattr(copy(), what)())
        pltpu.make_async_copy(wd_ref, dw_out, out_sem.at[0]).start()

    @pl.when(g == 2 * half - 1)
    def _():
        pltpu.make_async_copy(wd_ref, dw_out, out_sem.at[0]).wait()

    main = (wgu_ref.shape[1] - 128) // 2
    gu = dot(n_ref[0], wgu_ref[...])
    gh = dot(cot_ref[0], wd_ref[...])

    def parts(gate, up, grad):
        sig = 1.0 / (1.0 + jnp.exp(-gate))
        silu = gate * sig
        return silu * up, grad * up * sig * (1.0 + gate * (1.0 - sig)), grad * silu

    hid, g_gate, g_up = parts(gu[:, :main], gu[:, main : 2 * main], gh[:, :main])
    h_ref[0, :, :main] = hid.astype(BF)
    ggu_ref[0, :, :main] = g_gate.astype(BF)
    ggu_ref[0, :, main : 2 * main] = g_up.astype(BF)
    rest = gu[:, 2 * main :]
    hid, g_gate, g_up = parts(rest, pltpu.roll(rest, 64, 1), gh[:, main:])
    low = lax.broadcasted_iota(jnp.int32, hid.shape, 1) < 64
    h_ref[0, :, main:] = jnp.where(low, hid, 0.0).astype(BF)
    ggu_ref[0, :, 2 * main :] = jnp.where(low, g_gate, pltpu.roll(g_up, 64, 1)).astype(BF)
    part = dot(ggu_ref[0], wgu_ref[...], NT).astype(BF)

    @pl.when(g < half)
    def _():
        out1[0] = part

    @pl.when(g >= half)
    def _():
        out0[0] = part


def grads_in_kernel(n_seq, sc, ga_ref, wo_ref, qkv_ref, mixed_ref, den_ref, maps, gaug_ref, after_ref, total_ref, state):
    k, n = pl.program_id(0), pl.num_programs(0)
    i = n - 1 - k

    @pl.when(k == 0)
    def _():
        state[...] = jnp.zeros_like(state)

    qkv = qkv_ref[0]
    rows = qkv.shape[0]
    ch = Chunk(sc, n_seq, i, rows)
    qk = query_key(qkv)
    gm = dot(ga_ref[0], wo_ref[...])
    lane = lax.broadcasted_iota(jnp.int32, (rows, 128), 1)
    for h in range(2):
        qa, qb, _, _, _, _ = read_maps(maps, h)
        den = den_ref[0, :, h : h + 1]
        grad = gm[:, h * DV : (h + 1) * DV] / den
        delta = -jnp.sum(grad * mixed_ref[0, :, h * DV : (h + 1) * DV].astype(F32), axis=1, keepdims=True)
        gaug = jnp.concatenate([grad, jnp.where(lane == 0, delta, 0.0)], axis=1).astype(BF)
        gaug_ref[0, :, h * 2 * DV : (h + 1) * 2 * DV] = gaug
        after_ref[0, h] = state[h].astype(BF)
        feat = (dot(qk, qa) * dot(qk, qb) * ch.carried).astype(BF)
        new = dot(feat, gaug, TN) + ch.keep * state[h]
        state[h] = new
        total_ref[h] = new.astype(BF)


def grads_kernel(
    n_seq, slot, sc, qkv_ref, gaug_ref, before_ref, enter_ref, after_ref, leave_ref, maps, w_ref, out1, out0, dqkv_ref
):
    g = pl.program_id(0)
    half = pl.num_programs(0) // 2
    qkv = qkv_ref[0]
    rows = qkv.shape[0]
    ch = Chunk(sc, n_seq, slot(g) ^ sc[0], rows)
    group_last = sc[1] + pl.num_programs(0) * rows - 1
    alive = (ch.before_start < sc[1]).astype(F32)
    alive_after = (start_of(sc, n_seq, group_last) <= ch.last).astype(F32)
    qk = query_key(qkv)
    ones = one_column(qk, maps)
    causal = ch.causal()
    dqk = jnp.zeros((rows, 128), F32)
    for h in range(2):
        qa, qb, ka, kb, q_to_k, k_to_q = read_maps(maps, h)
        value = with_one(qkv[:, h * DV : (h + 1) * DV], ones)
        gaug = gaug_ref[0, :, h * 2 * DV : (h + 1) * 2 * DV]
        quarter = dot(qk, q_to_k).astype(BF)
        s = dot(quarter, qk, NT)
        w = jnp.where(causal, 1.0 + s + 0.5 * s * s, 0.0).astype(BF)
        ds = jnp.where(causal, dot(gaug, value, NT) * (1.0 + s), 0.0).astype(BF)
        dqk += dot(ds, dot(qk, k_to_q).astype(BF)) + dot(ds, quarter, TN)
        before = (before_ref[0, h].astype(F32) + alive * enter_ref[h].astype(F32)).astype(BF)
        after = (after_ref[0, h].astype(F32) + alive_after * leave_ref[h].astype(F32)).astype(BF)
        a, b = dot(qk, qa), dot(qk, qb)
        df = dot(gaug, before, NT) * ch.carried
        dqk += dot((df * b).astype(BF), qa, NT) + dot((df * a).astype(BF), qb, NT)
        a, b = dot(qk, ka), dot(qk, kb)
        df = dot(value, after, NT) * ch.tail
        dqk += dot((df * b).astype(BF), ka, NT) + dot((df * a).astype(BF), kb, NT)
        feat = (a * b * ch.tail).astype(BF)
        dv = dot(w, gaug[:, :DV], TN) + dot(feat, after[:, :DV])
        dqkv_ref[0, :, h * DV : (h + 1) * DV] = dv.astype(BF)
    lane = lax.broadcasted_iota(jnp.int32, dqk.shape, 1)
    dqkv_ref[0, :, 2 * DV :] = jnp.where(lane < LANE_ONE, dqk, 0.0).astype(BF)
    part = dot(dqkv_ref[0], w_ref[...], NT).astype(BF)

    @pl.when(g < half)
    def _():
        out1[0] = part

    @pl.when(g >= half)
    def _():
        out0[0] = part


class Place:
    def __init__(self):
        self.n = lax.axis_size("seq")
        self.groups = self.n // PLANE
        s = lax.axis_index("seq")
        self.s, self.z, self.p, self.c = s, s // PLANE, s % PLANE, lax.axis_index("head")

    def flip(self, v, bits):
        return lax.ppermute(v, "seq", [(s, s ^ bits) for s in range(self.n)])

    def core(self, v):
        return lax.ppermute(v, "head", [(0, 1), (1, 0)])

    def along(self, v, step, sources):
        pairs = [
            (s, s + step * PLANE)
            for s in range(self.n)
            if s // PLANE in sources and 0 <= s // PLANE + step < self.groups
        ]
        return lax.ppermute(v, "seq", pairs)

    def spread(self, pack):
        own = [lax.dynamic_index_in_dim(pack, self.p ^ j, 0, keepdims=False) for j in range(PLANE)]
        got = [own[0]] + [self.flip(own[j], j) for j in range(1, PLANE)]
        return [lax.select_n(self.p, *[got[i ^ q] for q in range(PLANE)]) for i in range(PLANE)]

    def gather_line(self, slab):
        up, down, top = [slab], [slab], self.groups
        for k in range(1, top):
            up.append(self.along(up[-1], 1, range(k - 1, top)))
            down.append(self.along(down[-1], -1, range(0, top - k + 1)))
        return [
            lax.select_n(self.z, *[up[q - i] if q >= i else down[i - q] for q in range(top)]) for i in range(top)
        ]

    def scatter_line(self, piece):
        top = self.groups
        total = piece(self.z).astype(F32)
        for step in (1, -1):
            got = None
            for k in range(1, top):
                far = top - k if step == 1 else k - top
                term = piece(jnp.clip(self.z + far, 0, top - 1))
                if got is not None:
                    term = (term.astype(F32) + got.astype(F32)).astype(BF)
                sources = range(0, k) if step == 1 else range(top - k, top)
                got = self.along(term, step, sources)
            if got is not None:
                total = total + got.astype(F32)
        return total

    def gather8(self, mine, other=None):
        cut = mine.shape[0] // 2
        mx, my = self.flip(mine, 1), self.flip(mine, 2)
        da, db = self.flip(my[:cut], 1), self.flip(mx[cut:], 2)
        other = self.core(mine) if other is None else other
        ox, oy, oda, odb = (self.core(v) for v in (mx, my, da, db))
        whole = jnp.concatenate([mine, other, mx, ox, my, oy, da, db, oda, odb], axis=0)
        return whole.reshape(2 * PLANE, mine.shape[0], mine.shape[1])

    def reduce8(self, other_half, own_half):
        total = own_half.astype(F32) + self.core(other_half).astype(F32)
        cut = total.shape[1] // 2
        a, b = total[:, :cut], total[:, cut:]
        got_x = self.flip(a[1::2].astype(BF), 1).astype(F32)
        got_y = self.flip(b[2:].astype(BF), 2).astype(F32)
        last_y = self.flip((a[2] + got_x[1]).astype(BF), 2).astype(F32)
        last_x = self.flip((b[1] + got_y[1]).astype(BF), 1).astype(F32)
        return jnp.concatenate([a[0] + got_x[0] + last_y, b[0] + got_y[0] + last_x], axis=0)

    def both(self, mine):
        other = self.core(mine)
        return jnp.concatenate(
            [lax.select_n(self.c, mine, other), lax.select_n(self.c, other, mine)], axis=0
        )


MESH = pl.DeviceIdType.MESH
N_SEMS = 160


def for_rows(count, body, block=32):
    def step(i, _):
        body(pl.ds(pl.multiple_of(i * block, block), block))
        return 0

    lax.fori_loop(0, count // block, step, 0)


class Copies:
    def __init__(self, items):
        self.items = items

    def each(self, what, conditions):
        for (copy, *_), cond in zip(self.items, conditions):
            if cond is None:
                getattr(copy(), what)()
            else:

                @pl.when(cond)
                def _(copy=copy):
                    getattr(copy(), what)()

    def start(self):
        self.each("start", [i[1] for i in self.items])
        return self

    def wait_send(self):
        self.each("wait_send", [i[1] for i in self.items])

    def wait_recv(self):
        self.each("wait_recv", [i[2] for i in self.items])


class Net:
    def __init__(self, n, sends, recvs, locals_):
        self.n, self.top = n, n // PLANE
        self.sends, self.recvs, self.locals_ = sends, recvs, locals_
        self.k = self.l = 0
        self.sent, self.local = [], []
        s, c = lax.axis_index("seq"), lax.axis_index("head")
        self.s, self.c = s, c
        self.z, self.p = lax.div(s, PLANE), lax.rem(s, PLANE)
        p = self.p
        self.part = [p, p + 1 - 2 * lax.rem(p, 2), p + 2 - 4 * lax.div(p, 2), 3 - p]
        base = s - p
        self.X, self.Y, self.D = ({"seq": base + q} for q in self.part[1:])
        self.C = {"head": 1 - c}
        self.up, self.down = {"seq": s + PLANE}, {"seq": s - PLANE}
        self.has_up, self.has_down = self.z < self.top - 1, self.z > 0

    def barrier(self, partners, line=False):
        sem = pltpu.get_barrier_semaphore()
        for to in partners:
            pl.semaphore_signal(sem, inc=1, device_id=to, device_id_type=MESH)
        count = len(partners)
        if line:
            for cond, to in ((self.has_up, self.up), (self.has_down, self.down)):

                @pl.when(cond)
                def _(to=to):
                    pl.semaphore_signal(sem, inc=1, device_id=to, device_id_type=MESH)

            count = count + self.has_up.astype(jnp.int32) + self.has_down.astype(jnp.int32)
        pl.semaphore_wait(sem, count)

    def barrier_hops(self, hops, back):
        sem = pltpu.get_barrier_semaphore()
        for hop in hops:
            for sign in (1, -1):
                at = self.z + sign * hop

                @pl.when((at >= 0) & (at < self.top))
                def _(sign=sign, hop=hop):
                    to = {"seq": self.s + sign * hop * PLANE}
                    pl.semaphore_signal(sem, inc=1, device_id=to, device_id_type=MESH)

        pl.semaphore_wait(sem, self.top - 1)

    def remote(self, src, dst, to, when=None, arrives=None):
        i = self.k
        self.k += 1
        assert i < N_SEMS

        def copy():
            return pltpu.make_async_remote_copy(
                src_ref=src(),
                dst_ref=dst(),
                send_sem=self.sends.at[i],
                recv_sem=self.recvs.at[i],
                device_id=to,
                device_id_type=MESH,
            )

        made = Copies([(copy, when, arrives)])
        self.sent.append(made)
        return made

    def put(self, src, dst, when=None):
        i = self.l
        self.l += 1
        assert i < N_SEMS

        def copy():
            return pltpu.make_async_copy(src(), dst(), self.locals_.at[i])

        class Local(Copies):
            def wait(self):
                self.each("wait", [when])

        made = Local([(copy, when, when)])
        made.start()
        self.local.append(made)
        return made

    def finish(self):
        for made in self.sent:
            made.wait_send()

    def step(self, k, src_up, src_down, dst_up, dst_down):
        z, top = self.z, self.top
        up = self.remote(src_up, dst_up, self.up, (z >= k - 1) & self.has_up, z >= k)
        down = self.remote(src_down, dst_down, self.down, (z + k <= top) & self.has_down, z + k <= top - 1)
        return Copies(up.items + down.items)


def rows_of(ref, block, rows):
    return ref.at[pl.ds(pl.multiple_of(block * rows, 16), rows)]


class Reduce:
    def scratch(slots, rows, width):
        cut = rows // 2
        return [
            pltpu.VMEM((slots, rows, width), BF),
            pltpu.VMEM((slots, rows, width), BF),
            pltpu.VMEM((2, cut, width), BF),
            pltpu.VMEM((2, cut, width), BF),
            pltpu.VMEM((2, cut, width), BF),
        ]

    def __init__(self, net, p1, p0, own, rc, rx, ry, r2):
        self.net, self.p1, self.p0 = net, p1, p0
        self.own, self.rc, self.rx, self.ry, self.r2 = own, rc, rx, ry, r2
        self.cut = rc.shape[1] // 2

    def piece(self, ref, j, hf):
        return ref.at[j, pl.ds(hf * self.cut, self.cut)]

    def send_core(self):
        net = self.net
        self.load = net.put(lambda: self.p0, lambda: self.own)
        self.core = {}
        for j, hf in ((3, 0), (3, 1), (1, 0), (2, 1), (2, 0), (1, 1), (0, 0), (0, 1)):
            self.core[j, hf] = net.remote(
                functools.partial(self.piece, self.p1, j, hf), functools.partial(self.piece, self.rc, j, hf), net.C
            ).start()
        self.load.wait()

    def add(self, j, hf):
        self.core[j, hf].wait_recv()
        rc, own = self.piece(self.rc, j, hf), self.piece(self.own, j, hf)

        def body(r):
            rc[r] = (rc[r].astype(F32) + own[r].astype(F32)).astype(BF)

        for_rows(self.cut, body)

    def first(self):
        net, made = self.net, {}
        for name, j, hf, land, to in (
            ("x1", 3, 0, self.rx.at[1], net.X),
            ("y1", 3, 1, self.ry.at[1], net.Y),
            ("x0", 1, 0, self.rx.at[0], net.X),
            ("y0", 2, 1, self.ry.at[0], net.Y),
        ):
            self.add(j, hf)
            made[name] = net.remote(functools.partial(self.piece, self.rc, j, hf), lambda land=land: land, to).start()
        self.made = made
        for j, hf in ((2, 0), (1, 1), (0, 0), (0, 1)):
            self.add(j, hf)

    def second(self):
        net = self.net
        for name, j, hf, land, i, to in (("x1", 2, 0, self.rx, 0, net.Y), ("y1", 1, 1, self.ry, 1, net.X)):
            self.made[name].wait_recv()
            at = self.piece(self.rc, j, hf)

            def body(r):
                at[r] = (at[r].astype(F32) + land[1, r].astype(F32)).astype(BF)

            for_rows(self.cut, body)
            self.made["last", hf] = net.remote(
                functools.partial(self.piece, self.rc, j, hf), lambda i=i: self.r2.at[i], to
            ).start()

    def last(self, hf, body):
        self.made["x0" if hf == 0 else "y0"].wait_recv()
        self.made["last", hf].wait_recv()
        land = self.rx if hf == 0 else self.ry

        def step(i, _):
            r = pl.ds(pl.multiple_of(i * 32, 32), 32)
            at = pl.ds(pl.multiple_of(hf * self.cut + i * 32, 32), 32)
            total = self.rc[0, at].astype(F32) + land[0, r].astype(F32) + self.r2[hf, r].astype(F32)
            body(at, total)
            return 0

        lax.fori_loop(0, self.cut // 32, step, 0)


class Gather:
    def __init__(self, net, out, rows):
        self.net, self.out, self.rows, self.cut = net, out, rows, rows // 2

    def half(self, ref, slot, hf):
        return ref.at[slot, pl.ds(hf * self.cut, self.cut)]

    def pass_on(self, src, slot, hf, to):
        return self.net.remote(src, functools.partial(self.half, self.out, slot, hf), to).start()

    def send(self, hf, src):
        to, slot = (self.net.Y, 4) if hf == 0 else (self.net.X, 2)
        setattr(self, f"on{hf}", self.pass_on(src, slot, hf, to))

    def send_rest(self, srcs, core=True):
        net = self.net
        self.late = [self.pass_on(srcs[0], 2, 0, net.X), self.pass_on(srcs[1], 4, 1, net.Y)]
        self.core = [self.pass_on(srcs[hf], 1, hf, net.C) for hf in (0, 1)] if core else []

    def forward(self):
        net, out = self.net, self.out
        at = lambda slot, hf: functools.partial(self.half, out, slot, hf)
        self.on0.wait_recv()
        self.far = [self.pass_on(at(4, 0), 6, 0, net.X)]
        self.on1.wait_recv()
        self.far.append(self.pass_on(at(2, 1), 6, 1, net.Y))
        self.core.append(self.pass_on(at(4, 0), 5, 0, net.C))
        self.core.append(self.pass_on(at(2, 1), 3, 1, net.C))

    def across(self):
        net, out = self.net, self.out
        at = lambda slot, hf: functools.partial(self.half, out, slot, hf)
        self.late[0].wait_recv()
        self.core.append(self.pass_on(at(2, 0), 3, 0, net.C))
        self.late[1].wait_recv()
        self.core.append(self.pass_on(at(4, 1), 5, 1, net.C))

    def finish(self):
        net, out = self.net, self.out
        at = lambda slot, hf: functools.partial(self.half, out, slot, hf)
        for hf in (0, 1):
            self.far[hf].wait_recv()
            self.core.append(self.pass_on(at(6, hf), 7, hf, net.C))
        for copy in self.core:
            copy.wait_recv()


class ToParts:
    def __init__(self, net, pack, rows):
        self.own = net.put(lambda: pack.at[net.p], lambda: rows(net.p))
        self.sent = [
            net.remote(functools.partial(lambda j: pack.at[net.part[j]], j), lambda: rows(net.p), to).start()
            for j, to in ((1, net.X), (2, net.Y), (3, net.D))
        ]

    def wait(self):
        self.own.wait()
        for copy in self.sent:
            copy.wait_recv()


def start_kernel(n, x, ap, gp, dp, x_all, aw, g0, g_up, g_down, d0, sends, recvs, locals_):
    net = Net(n, sends, recvs, locals_)
    z, c, top = net.z, net.c, net.top
    db = ap.shape[1]
    slab = PLANE * db
    half = x.shape[0] // 2
    cut = half // 2
    net.barrier((net.X, net.Y, net.D, net.C), line=True)
    attn = ToParts(net, ap, lambda q: rows_of(aw, z * PLANE + q, db))
    gate_up = ToParts(net, gp, lambda q: rows_of(g0, q, db))
    gather = Gather(net, x_all, half)
    mine = lambda hf: functools.partial(rows_of, x, c * 2 + hf, cut)
    net.put(lambda: rows_of(x, c, half), lambda: x_all.at[0])
    net.put(lambda: rows_of(x, 1 - c, half), lambda: x_all.at[1])
    gather.send(0, mine(0))
    gather.send(1, mine(1))
    gather.send_rest([mine(0), mine(1)], core=False)
    attn.wait()

    def attn_step(k):
        up, down = (lambda: rows_of(aw, z - k + 1, slab)), (lambda: rows_of(aw, z + k - 1, slab))
        return net.step(k, up, down, up, down).start()

    line = attn_step(1)
    gather.forward()
    down_part = ToParts(net, dp, lambda q: rows_of(d0, q, db))
    for k in range(2, top):
        line.wait_recv()
        line = attn_step(k)
        if k == 2:
            gather.across()
    gate_up.wait()
    gu = net.step(1, lambda: g0, lambda: g0, lambda: g_up, lambda: g_down).start()
    line.wait_recv()
    gather.finish()
    down_part.wait()
    gu.wait_recv()
    for made in net.local[1:]:
        if made not in (attn.own, gate_up.own, down_part.own):
            made.wait()
    net.finish()


def norm_kernel(
    n, p1, p0, x_ref, gain_ref, gu2, gd2, du1, dd1, cot, cx, cy, ca, cb,
    out, resid_ref, gw, dw, cot_all, own, rc, rx, ry, r2, mine, sends, recvs, locals_,
):
    net = Net(n, sends, recvs, locals_)
    z, c, top = net.z, net.c, net.top
    slab = gu2.shape[0]
    net.barrier((net.X, net.Y, net.C), line=True)
    red = Reduce(net, p1, p0, own, rc, rx, ry, r2)
    red.send_core()
    half, cut = rc.shape[1], red.cut

    gu_line = net.step(3, lambda: gu2, lambda: gd2, lambda: rows_of(gw, z - 2, slab), lambda: rows_of(gw, z + 2, slab))
    gu_line.start()
    d_line = net.step(2, lambda: du1, lambda: dd1, lambda: rows_of(dw, z - 1, slab), lambda: rows_of(dw, z + 1, slab))
    d_line.start()
    red.first()
    kept = [
        net.put(lambda: rows_of(cot, c, half), lambda: cot_all.at[0]),
        net.put(lambda: rows_of(cot, 1 - c, half), lambda: cot_all.at[1]),
        net.put(lambda: cx, lambda: cot_all.at[2]),
        net.put(lambda: cy, lambda: cot_all.at[4]),
        net.put(lambda: ca, lambda: cot_all.at[6, pl.ds(0, cut)]),
        net.put(lambda: cb, lambda: cot_all.at[6, pl.ds(cut, cut)]),
    ]
    crossing = [
        net.remote(lambda: cx, lambda: cot_all.at[3], net.C).start(),
        net.remote(lambda: cy, lambda: cot_all.at[5], net.C).start(),
        net.remote(lambda: ca, lambda: cot_all.at[7, pl.ds(0, cut)], net.C).start(),
        net.remote(lambda: cb, lambda: cot_all.at[7, pl.ds(cut, cut)], net.C).start(),
    ]
    red.second()

    def norm(at, total):
        resid = x_ref[at].astype(F32) + total
        resid_ref[at] = resid
        inv = lax.rsqrt(jnp.mean(resid * resid, axis=-1, keepdims=True) + 1e-05)
        mine[at] = (resid * inv * gain_ref[...]).astype(BF)

    gather = Gather(net, out, half)
    part = lambda hf: functools.partial(rows_of, mine, hf, cut)
    for hf in (0, 1):
        red.last(hf, norm)
        gather.send(hf, part(hf))
    gather.send_rest([part(0), part(1)])
    kept.append(net.put(lambda: mine, lambda: out.at[0]))

    def gu_step(k):
        up, down = (lambda: rows_of(gw, z - k + 1, slab)), (lambda: rows_of(gw, z + k - 1, slab))
        return net.step(k, up, down, up, down).start()

    def d_step(k):
        up, down = (lambda: rows_of(dw, z - k + 1, slab)), (lambda: rows_of(dw, z + k - 1, slab))
        return net.step(k, up, down, up, down).start()

    for k in range(3, top):
        d_line.wait_recv()
        d_line = d_step(k)
        if k + 1 < top:
            gu_line.wait_recv()
            gu_line = gu_step(k + 1)
    gather.forward()
    gather.across()
    gather.finish()
    gu_line.wait_recv()
    d_line.wait_recv()
    for copy in crossing:
        copy.wait_recv()
    for made in kept:
        made.wait()
    net.finish()


class LineSum:
    def scratch(top, slab, width):
        return [pltpu.VMEM((2, top, slab, width), BF), pltpu.VMEM((2, slab, width), BF)]

    def __init__(self, net, grads, slab, land, term):
        self.net, self.grads, self.land, self.term, self.slab = net, grads, land, term, slab
        z, top = net.z, net.top
        self.before = (z > 0, z < top - 1)
        self.after = (z < top - 1, z > 0)

    def block(self, i):
        return rows_of(self.grads, i, self.slab)

    def fetch(self, k):
        z, top, net = self.net.z, self.net.top, self.net
        self.has = ((z <= k - 1) & self.after[0], (z >= top - k) & self.after[1])
        self.got = []
        for d, i in ((0, z + top - k), (1, z - top + k)):
            src = functools.partial(self.block, i)
            land = lambda d=d: self.land.at[d, k - 1]
            term = lambda d=d: self.term.at[d]
            self.got.append(net.put(src, term, self.has[d] & self.before[d]))
            self.got.append(net.put(src, land, self.has[d] & jnp.logical_not(self.before[d])))

    def send(self, k):
        net, z, top = self.net, self.net.z, self.net.top
        for got in self.got:
            got.wait()
        if k > 1:
            self.arriving.wait_recv()
        for d in (0, 1):

            @pl.when(self.has[d] & self.before[d])
            def _(d=d):
                land, term = self.land.at[d, k - 1], self.term.at[d]

                def body(r):
                    land[r] = (land[r].astype(F32) + term[r].astype(F32)).astype(BF)

                for_rows(self.slab, body)

        arrives = (self.before[0] & (z <= k), self.before[1] & (z >= top - 1 - k))
        items = []
        for d, to in ((0, net.up), (1, net.down)):
            src = lambda d=d: self.land.at[d, k - 1]
            dst = lambda d=d: self.land.at[d, k]
            items += net.remote(src, dst, to, self.has[d], arrives[d]).items
        self.arriving = Copies(items).start()

    def fetch_own(self):
        self.own = self.net.put(lambda: self.block(self.net.z), lambda: self.term.at[0])

    def total(self, out):
        self.own.wait()
        self.arriving.wait_recv()
        last = self.net.top - 1
        term, up, down = self.term.at[0], self.land.at[0, last], self.land.at[1, last]

        def run(*refs):
            def body(r):
                out[r] = sum(ref[r].astype(F32) for ref in refs).astype(BF)

            for_rows(self.slab, body)

        below, above = self.before
        pl.when(below & above)(lambda: run(term, up, down))
        pl.when(below & jnp.logical_not(above))(lambda: run(term, up))
        pl.when(above & jnp.logical_not(below))(lambda: run(term, down))


def back_kernel(
    n, p1, p0, resid_ref, cot_ref, gain_ref, gu_grad,
    out, grad_resid_ref, gu_sum, own, rc, rx, ry, r2, mine, land, term, sends, recvs, locals_,
):
    net = Net(n, sends, recvs, locals_)
    top = net.top
    slab = gu_sum.shape[0]
    net.barrier((net.X, net.Y, net.C), line=True)
    line = LineSum(net, gu_grad, slab, land, term)
    red = Reduce(net, p1, p0, own, rc, rx, ry, r2)
    line.fetch(1)
    red.send_core()
    line.send(1)
    red.first()
    line.fetch(2)
    red.second()
    line.send(2)
    half, cut = rc.shape[1], red.cut

    def norm_back(at, total):
        resid = resid_ref[at]
        inv = lax.rsqrt(jnp.mean(resid * resid, axis=-1, keepdims=True) + 1e-05)
        grad = cot_ref[at].astype(F32) + rms_back(total, resid * inv, inv, gain_ref[...])
        grad_resid_ref[at] = grad
        mine[at] = grad.astype(BF)

    gather = Gather(net, out, half)
    part = lambda hf: functools.partial(rows_of, mine, hf, cut)
    for hf in (0, 1):
        red.last(hf, norm_back)
        gather.send(hf, part(hf))
    gather.send_rest([part(0), part(1)])
    kept = net.put(lambda: mine, lambda: out.at[0])
    line.fetch(3)
    gather.forward()
    gather.across()
    line.send(3)
    gather.finish()
    for k in range(4, top):
        line.fetch(k)
        line.send(k)
    line.fetch_own()
    line.total(gu_sum)
    kept.wait()
    net.finish()


def final_kernel(
    n, p1, p0, at_grad, gu_sum, d_sum,
    sum_ref, gu_out, d_out, at_out, own, rc, rx, ry, r2, mine, land, term, at_sum, sends, recvs, locals_,
):
    net = Net(n, sends, recvs, locals_)
    top, c = net.top, net.c
    slab = at_sum.shape[0]
    db = slab // PLANE
    net.barrier((net.X, net.Y, net.D, net.C), line=True)
    line = LineSum(net, at_grad, slab, land, term)
    red = Reduce(net, p1, p0, own, rc, rx, ry, r2)
    line.fetch(1)
    red.send_core()
    line.send(1)
    red.first()
    line.fetch(2)
    red.second()
    line.send(2)
    gu_parts = PartsBack(net, gu_sum, gu_out, db)
    d_parts = PartsBack(net, d_sum, d_out, db)
    half, cut = rc.shape[1], red.cut
    line.fetch(3)

    def keep(at, total):
        mine[at] = total.astype(BF)

    across = []
    for hf in (0, 1):
        red.last(hf, keep)
        part = functools.partial(rows_of, mine, hf, cut)
        across.append(net.remote(part, lambda hf=hf: sum_ref.at[c, pl.ds(hf * cut, cut)], net.C).start())
    kept = net.put(lambda: mine, lambda: sum_ref.at[c])
    line.send(3)
    for k in range(4, top):
        line.fetch(k)
        line.send(k)
    line.fetch_own()
    line.total(at_sum)
    at_parts = PartsBack(net, at_sum, at_out, db)
    for parts in (gu_parts, d_parts, at_parts):
        parts.wait()
    for copy in across:
        copy.wait_recv()
    kept.wait()
    net.finish()


class PartsBack:
    def __init__(self, net, src, out, rows):
        self.own = net.put(lambda: rows_of(src, net.p, rows), lambda: out.at[net.p])
        self.sent = [
            net.remote(functools.partial(lambda j: rows_of(src, net.part[j], rows), j), lambda: out.at[net.p], to).start()
            for j, to in ((1, net.X), (2, net.Y), (3, net.D))
        ]

    def wait(self):
        self.own.wait()
        for copy in self.sent:
            copy.wait_recv()


def cost(flops, nbytes):
    return pl.CostEstimate(flops=int(flops), bytes_accessed=int(nbytes), transcendentals=0)


def rms_parts(rows):
    return lax.rsqrt(jnp.mean(rows * rows, axis=-1, keepdims=True) + 1e-05)


def rms_back(grad_normed, x_hat, inv_rms, gain_vec):
    grad_hat = grad_normed * gain_vec
    return inv_rms * (grad_hat - x_hat * jnp.mean(grad_hat * x_hat, axis=-1, keepdims=True))


def split_hidden(w):
    rows, cols = w.shape
    main = cols // PLANE // 128 * 128
    rest = (cols - PLANE * main) // PLANE
    first = w[:, : PLANE * main].reshape(rows, PLANE, main)
    return first.transpose(1, 0, 2), w[:, PLANE * main :].reshape(rows, PLANE, rest).transpose(1, 0, 2)


def shards(
    layer_input,
    seq_lengths,
    gain_attn,
    w_query,
    w_key,
    w_value,
    w_out,
    gain_mlp,
    w_gate,
    w_up,
    w_down,
    cotangent,
):
    me = Place()
    rows, width = layer_input.shape
    half_rows = rows // 2
    slots = 2 * PLANE
    group_rows = PLANE * rows
    n_seq = seq_lengths.shape[0]
    db = w_query.shape[0]
    hidden = w_down.shape[0]
    main = hidden // PLANE // 128 * 128
    rest = hidden // PLANE - main
    assert H == slots * 2 and rest == 64
    own8 = me.p * 2 + me.c

    k = jnp.arange(n_seq)
    starts = jnp.sum(jnp.where(k[None, :] < k[:, None], seq_lengths[None, :], 0), axis=1)
    first = me.z * group_rows
    sc = jnp.concatenate([jnp.stack([own8, first]).astype(jnp.int32), starts.astype(jnp.int32)])
    maps = feature_maps()

    def slot_first_other(g):
        return (g % PLANE) * 2 + 1 - g // PLANE

    top = me.groups
    slab = PLANE * db
    cut = half_rows // 2
    anywhere, in_vmem = pl.BlockSpec(memory_space=pl.ANY), pl.BlockSpec(memory_space=pltpu.VMEM)
    sems = [pltpu.SemaphoreType.DMA((N_SEMS,))] * 3
    shape = lambda *dims: jax.ShapeDtypeStruct(dims, BF)

    def net_call(kernel, name, cid, args, in_specs, outs, out_specs, scratch):
        return pl.pallas_call(
            functools.partial(kernel, me.n),
            in_specs=in_specs,
            out_specs=out_specs,
            out_shape=outs,
            scratch_shapes=[*scratch, *sems],
            compiler_params=pltpu.CompilerParams(collective_id=cid, has_side_effects=True, vmem_limit_bytes=VMEM),
            cost_estimate=cost(10**8, 10**8),
            name=name,
        )(*args)

    def by_part(w, parts=PLANE):
        return w.reshape(w.shape[0], parts, w.shape[1] // parts).transpose(1, 0, 2)

    gains = jnp.stack([gain_attn, gain_mlp], axis=1)
    fill = jnp.concatenate([gains, jnp.zeros((db, 62), BF)], axis=1)
    attn_pack = jnp.concatenate(
        [by_part(w_value), by_part(w_query), by_part(w_key), jnp.broadcast_to(fill, (PLANE, db, 64)), by_part(w_out.T)],
        axis=2,
    )
    g_main, g_rest = split_hidden(w_gate)
    u_main, u_rest = split_hidden(w_up)
    gu_pack = jnp.concatenate([g_main, u_main, g_rest, u_rest], axis=2)
    d_main, d_rest = split_hidden(w_down.T)
    down_pack = jnp.concatenate([d_main, d_rest, jnp.zeros((PLANE, db, 64), BF)], axis=2)
    wide = 2 * main + 2 * rest
    tall = main + 128

    def my_half(v):
        return lax.dynamic_slice_in_dim(v, me.c * half_rows, half_rows, 0)

    x_all, attn_w, gu0, gu_up1, gu_down1, d0 = net_call(
        start_kernel,
        "start",
        1,
        (layer_input, attn_pack, gu_pack, down_pack),
        [in_vmem] * 4,
        [
            shape(slots, half_rows, width),
            shape(width, 5 * DV),
            shape(slab, wide),
            shape(slab, wide),
            shape(slab, wide),
            shape(slab, tall),
        ],
        [anywhere] * 6,
        [],
    )
    gu_up2 = me.along(gu_up1, 1, range(1, top))
    gu_down2 = me.along(gu_down1, -1, range(0, top - 1))
    d_up1 = me.along(d0, 1, range(top))
    d_down1 = me.along(d0, -1, range(top))
    cot_mine = my_half(cotangent)
    cot_x, cot_y = me.flip(cot_mine, 1), me.flip(cot_mine, 2)
    cot_a, cot_b = me.flip(cot_y[:cut], 1), me.flip(cot_x[cut:], 2)

    w_qkv, w_o = attn_w[:, : 3 * DV], attn_w[:, 3 * DV :]
    gain_one = attn_w[:, 2 * DV + 64].astype(F32)[None, :]
    gain_two = attn_w[:, 2 * DV + 65].astype(F32)[None, :]

    params = pltpu.CompilerParams(dimension_semantics=("arbitrary",), vmem_limit_bytes=VMEM)
    row_block = lambda cols: pl.BlockSpec((1, half_rows, cols), lambda g: (g, 0, 0))
    whole = lambda *shape: pl.BlockSpec(shape, lambda *_: (0,) * len(shape))

    normed, qkv = pl.pallas_call(
        project_kernel,
        grid=(slots,),
        in_specs=[row_block(width), whole(1, width), whole(width, 3 * DV)],
        out_specs=[row_block(width), row_block(3 * DV)],
        out_shape=[
            jax.ShapeDtypeStruct((slots, half_rows, width), BF),
            jax.ShapeDtypeStruct((slots, half_rows, 3 * DV), BF),
        ],
        compiler_params=params,
        cost_estimate=cost(2 * group_rows * width * 3 * DV, 4 * group_rows * width),
        name="project",
    )(x_all, gain_one, w_qkv)

    map_spec = whole(*maps.shape)
    state_spec = whole(2, FE, 2 * DV)
    state_shape = jax.ShapeDtypeStruct((2, FE, 2 * DV), BF)
    states_shape = jax.ShapeDtypeStruct((slots, 2, FE, 2 * DV), BF)

    def in_order(cols):
        return pl.BlockSpec((1, half_rows, cols), lambda i, s: (i ^ s[0], 0, 0))

    before, total = pl.pallas_call(
        functools.partial(states_kernel, n_seq),
        grid_spec=pltpu.PrefetchScalarGridSpec(
            num_scalar_prefetch=1,
            grid=(slots,),
            in_specs=[in_order(3 * DV), map_spec],
            out_specs=[pl.BlockSpec((1, 2, FE, 2 * DV), lambda i, s: (i, 0, 0, 0)), state_spec],
            scratch_shapes=[pltpu.VMEM((2, FE, 2 * DV), F32)],
        ),
        out_shape=[states_shape, state_shape],
        compiler_params=params,
        cost_estimate=cost(slots * 2e8, 2**21),
        name="states",
    )(sc, qkv, maps)

    def start_at(pos):
        return jnp.max(jnp.where(starts <= pos, starts, 0))

    reach = start_at(first - 1)
    enter = jnp.zeros((2, FE, 2 * DV), F32)
    for hop in range(1, top):
        got = me.along(total, hop, range(top)).astype(F32)
        live = (me.z >= hop) & (reach < first - (hop - 1) * group_rows)
        enter = enter + jnp.where(live, got, 0.0)
    enter = enter.astype(BF)

    def any_order(cols):
        return pl.BlockSpec((1, half_rows, cols), lambda g, s: (slot_first_other(g), 0, 0))

    def any_state(g, s):
        return (slot_first_other(g) ^ s[0], 0, 0, 0)

    part_specs = [
        pl.BlockSpec((1, half_rows, width), lambda g, *_: (jnp.minimum(g, PLANE - 1), 0, 0)),
        pl.BlockSpec((1, half_rows, width), lambda g, *_: (jnp.maximum(g - PLANE, 0), 0, 0)),
    ]
    part_shapes = [jax.ShapeDtypeStruct((PLANE, half_rows, width), BF)] * 2
    attn_other, attn_own, mixed, den = pl.pallas_call(
        functools.partial(attend_kernel, n_seq, slot_first_other),
        grid_spec=pltpu.PrefetchScalarGridSpec(
            num_scalar_prefetch=1,
            grid=(slots,),
            in_specs=[
                any_order(3 * DV),
                pl.BlockSpec((1, 2, FE, 2 * DV), any_state),
                state_spec,
                map_spec,
                whole(width, 2 * DV),
            ],
            out_specs=[*part_specs, any_order(2 * DV), any_order(128)],
        ),
        out_shape=[
            *part_shapes,
            jax.ShapeDtypeStruct((slots, half_rows, 2 * DV), BF),
            jax.ShapeDtypeStruct((slots, half_rows, 128), F32),
        ],
        compiler_params=params,
        cost_estimate=cost(slots * 8e8, 2**24),
        name="attend",
    )(sc, qkv, before, enter, maps, w_o)

    reduce_scratch = Reduce.scratch(PLANE, half_rows, width)
    mine_scratch = pltpu.VMEM((half_rows, width), BF)
    rows_f32 = jax.ShapeDtypeStruct((half_rows, width), F32)
    normed_mlp, resid, gu_far, d_far, cot_all = net_call(
        norm_kernel,
        "norm",
        2,
        (
            attn_other, attn_own, my_half(layer_input), gain_two, gu_up2, gu_down2, d_up1, d_down1,
            cotangent, cot_x, cot_y, cot_a, cot_b,
        ),
        [anywhere, anywhere, in_vmem, in_vmem, *[anywhere] * 4, *[in_vmem] * 5],
        [shape(slots, half_rows, width), rows_f32, shape(width, wide), shape(width, tall), shape(slots, half_rows, width)],
        [anywhere, in_vmem, anywhere, anywhere, anywhere],
        [*reduce_scratch, mine_scratch],
    )

    hid, grad_gu, gn_other, gn_own, down_w = pl.pallas_call(
        functools.partial(mlp_kernel, top),
        grid=(slots,),
        in_specs=[
            pl.BlockSpec((1, half_rows, width), lambda g: (slot_first_other(g), 0, 0)),
            pl.BlockSpec((1, half_rows, width), lambda g: (slot_first_other(g), 0, 0)),
            *[anywhere] * 10,
        ],
        out_specs=[
            pl.BlockSpec((1, half_rows, tall), lambda g: (slot_first_other(g), 0, 0)),
            pl.BlockSpec((1, half_rows, wide), lambda g: (slot_first_other(g), 0, 0)),
            *part_specs,
            anywhere,
        ],
        out_shape=[shape(slots, half_rows, tall), shape(slots, half_rows, wide), *part_shapes, shape(width, tall)],
        scratch_shapes=[
            pltpu.VMEM((width, wide), BF),
            pltpu.VMEM((width, tall), BF),
            pltpu.SemaphoreType.DMA((4 * top,)),
            pltpu.SemaphoreType.DMA((1,)),
        ],
        compiler_params=params,
        cost_estimate=cost(2 * group_rows * width * (2 * wide + tall), 2**25),
        name="mlp",
    )(normed_mlp, cot_all, gu0, gu_up1, gu_down1, gu_up2, gu_down2, gu_far, d0, d_up1, d_down1, d_far)

    def flat(v):
        return v.reshape(slots * half_rows, v.shape[2])

    gu_grad = dot(flat(normed_mlp), flat(grad_gu), TN).astype(BF)
    grad_attn, grad_resid, gu_sum = net_call(
        back_kernel,
        "back",
        3,
        (gn_other, gn_own, resid, cot_mine, gain_two, gu_grad),
        [anywhere, anywhere, in_vmem, in_vmem, in_vmem, anywhere],
        [shape(slots, half_rows, width), rows_f32, shape(slab, wide)],
        [anywhere, in_vmem, in_vmem],
        [*reduce_scratch, mine_scratch, *LineSum.scratch(top, slab, wide)],
    )
    down_grad = dot(flat(cot_all), flat(hid), TN).astype(BF)
    lo = dot(flat(hid), down_w, NT).astype(BF).reshape(PLANE, 2, half_rows, width)
    mlp_sum = me.reduce8(lo[:, 1], lo[:, 0])
    layer_out = me.both((resid + mlp_sum).astype(BF))

    def reverse(cols):
        return pl.BlockSpec((1, half_rows, cols), lambda k, s: ((slots - 1 - k) ^ s[0], 0, 0))

    gaug, after, back_total = pl.pallas_call(
        functools.partial(grads_in_kernel, n_seq),
        grid_spec=pltpu.PrefetchScalarGridSpec(
            num_scalar_prefetch=1,
            grid=(slots,),
            in_specs=[reverse(width), whole(width, 2 * DV), reverse(3 * DV), reverse(2 * DV), reverse(128), map_spec],
            out_specs=[
                reverse(4 * DV),
                pl.BlockSpec((1, 2, FE, 2 * DV), lambda k, s: (slots - 1 - k, 0, 0, 0)),
                state_spec,
            ],
            scratch_shapes=[pltpu.VMEM((2, FE, 2 * DV), F32)],
        ),
        out_shape=[jax.ShapeDtypeStruct((slots, half_rows, 4 * DV), BF), states_shape, state_shape],
        compiler_params=params,
        cost_estimate=cost(slots * 8e8, 2**24),
        name="grads_in",
    )(sc, grad_attn, w_o, qkv, mixed, den, maps)

    leave = jnp.zeros((2, FE, 2 * DV), F32)
    for hop in range(1, top):
        got = me.along(back_total, -hop, range(top)).astype(F32)
        other_first = first + hop * group_rows
        live = (me.z + hop < top) & (start_at(other_first - 1) < first + group_rows)
        leave = leave + jnp.where(live, got, 0.0)
    leave = leave.astype(BF)

    ga_other, ga_own, dqkv = pl.pallas_call(
        functools.partial(grads_kernel, n_seq, slot_first_other),
        grid_spec=pltpu.PrefetchScalarGridSpec(
            num_scalar_prefetch=1,
            grid=(slots,),
            in_specs=[
                any_order(3 * DV),
                any_order(4 * DV),
                pl.BlockSpec((1, 2, FE, 2 * DV), any_state),
                state_spec,
                pl.BlockSpec((1, 2, FE, 2 * DV), any_state),
                state_spec,
                map_spec,
                whole(width, 3 * DV),
            ],
            out_specs=[*part_specs, any_order(3 * DV)],
        ),
        out_shape=[*part_shapes, jax.ShapeDtypeStruct((slots, half_rows, 3 * DV), BF)],
        compiler_params=params,
        cost_estimate=cost(slots * 16e8, 2**24),
        name="grads",
    )(sc, qkv, gaug, before, enter, after, leave, maps, w_qkv)

    qkv_grad = dot(flat(normed), flat(dqkv), TN).astype(BF)
    o_grad = dot(flat(grad_attn), flat(mixed), TN).astype(BF)
    attn_grad = jnp.concatenate([qkv_grad, o_grad], axis=1)

    def row_piece(v):
        return lambda i: lax.dynamic_slice_in_dim(v, i * slab, slab, 0)

    d_sum = me.scatter_line(row_piece(down_grad)).astype(BF)
    grad_normed_both, gu_parts, down_parts, attn_parts = net_call(
        final_kernel,
        "final",
        4,
        (ga_other, ga_own, attn_grad, gu_sum, d_sum),
        [anywhere, anywhere, anywhere, in_vmem, in_vmem],
        [
            shape(2, half_rows, width),
            shape(PLANE, db, wide),
            shape(PLANE, db, tall),
            shape(PLANE, db, 5 * DV),
        ],
        [anywhere] * 4,
        [*reduce_scratch, mine_scratch, *LineSum.scratch(top, slab, 5 * DV), pltpu.VMEM((slab, 5 * DV), BF)],
    )
    grad_normed_both = grad_normed_both.reshape(rows, width).astype(F32)
    grad_resid_both = me.both(grad_resid)
    x_float = layer_input.astype(F32)
    inv_one = rms_parts(x_float)
    input_grad = grad_resid_both + rms_back(grad_normed_both, x_float * inv_one, inv_one, gain_one)

    def cols(parts, a, b):
        return [parts[q, :, a:b].astype(F32) for q in range(PLANE)]

    gate_grad = jnp.concatenate(cols(gu_parts, 0, main) + cols(gu_parts, 2 * main, 2 * main + rest), axis=1)
    up_grad = jnp.concatenate(cols(gu_parts, main, 2 * main) + cols(gu_parts, 2 * main + rest, wide), axis=1)
    down_out = jnp.concatenate(cols(down_parts, 0, main) + cols(down_parts, main, main + rest), axis=1).T
    value_grad = jnp.concatenate(cols(attn_parts, 0, 2 * DV), axis=1)
    query_grad = jnp.concatenate(cols(attn_parts, 2 * DV, 2 * DV + 2 * FD), axis=1)
    key_grad = jnp.concatenate(cols(attn_parts, 2 * DV + 2 * FD, 2 * DV + 4 * FD), axis=1)
    out_grad = jnp.concatenate(cols(attn_parts, 3 * DV, 5 * DV), axis=1).T

    def along_cols(*pairs):
        return sum(jnp.sum(w.astype(F32) * grad, axis=1) for w, grad in pairs)

    gain_parts = jnp.stack(
        [
            along_cols((w_query, query_grad), (w_key, key_grad), (w_value, value_grad)),
            along_cols((w_gate, gate_grad), (w_up, up_grad)),
        ]
    )
    gain_sums = gain_parts + me.core(gain_parts)
    gain_one_grad = gain_sums[0] / gain_attn.astype(F32)
    gain_two_grad = gain_sums[1] / gain_mlp.astype(F32)

    den2 = den[:, :, :2]
    ends = jnp.stack([-jnp.min(den2), jnp.max(den2)])
    ends = jnp.broadcast_to(ends[:, None], (2, 128))
    ends = jnp.maximum(ends, me.core(ends))
    ends = jnp.maximum(ends, me.flip(ends, 1))
    ends = jnp.maximum(ends, me.flip(ends, 2))
    best = ends
    for hop in range(1, top):
        for step in (hop, -hop):
            got = me.along(ends, step, range(top))
            ok = (me.z - step >= 0) & (me.z - step < top)
            best = jnp.where(ok, jnp.maximum(best, got), best)
    den_stats = jnp.stack([jnp.log(-best[0, 0]), jnp.log(best[1, 0])])

    return (
        layer_out,
        input_grad,
        gain_one_grad,
        query_grad,
        key_grad,
        value_grad,
        out_grad,
        gain_two_grad,
        gate_grad,
        up_grad,
        down_out,
        den_stats,
    )


def solution(mesh):
    return jax.shard_map(
        shards,
        mesh=mesh,
        in_specs=(
            P("seq", None),
            P(),
            P("seq"),
            P("seq", "head"),
            P("seq", "head"),
            P("seq", "head"),
            P("head", "seq"),
            P("seq"),
            P("seq", "head"),
            P("seq", "head"),
            P("head", "seq"),
            P("seq", None),
        ),
        out_specs=(
            P("seq", None),
            P("seq", None),
            P("seq"),
            P("seq", "head"),
            P("seq", "head"),
            P("seq", "head"),
            P("head", "seq"),
            P("seq"),
            P("seq", "head"),
            P("seq", "head"),
            P("head", "seq"),
            P(),
        ),
        check_vma=False,
    )
```
